256 devices in a mesh: dp: 8 (over z), seq: 16 (over y, x_lo, core), tile: 2 (over x_hi).
Axes of the slice: x: 4 (x_hi: 2, x_lo: 2; x = x_hi * 2 + x_lo), y: 4, z: 8, core: 2. Of those that a mesh axis runs over, the one named last changes fastest.
Arguments:
- queries: bfloat16 [8, 3072, 1536], P('dp', 'seq', 'tile'), may hold values from -5.318296 to 5.318296
- key_vectors: bfloat16 [8, 3072, 1536], P('dp', 'seq', 'tile'), may hold values from -5.318296 to 5.318296
- value_vectors: bfloat16 [8, 3072, 1536], P('dp', 'seq', 'tile'), may hold values from -6 to 6
- residual: bfloat16 [8, 3072, 1536], P('dp', 'seq', 'tile'), may hold values from -2 to 2
- out_weight: bfloat16 [1536, 1536], P('tile'), may hold values from -0.625 to 0.625
- cotangent: bfloat16 [8, 3072, 1536], P('dp', 'seq', 'tile'), may hold values from -6 to 6
Outputs:
- layer_out: bfloat16 [8, 3072, 1536], P('dp', 'seq', 'tile')
- grad_queries: bfloat16 [8, 3072, 1536], P('dp', 'seq', 'tile')
- grad_keys: bfloat16 [8, 3072, 1536], P('dp', 'seq', 'tile')
- grad_values: bfloat16 [8, 3072, 1536], P('dp', 'seq', 'tile')
- projection_weight_gradient: float32 [1536, 1536], P('tile')
The draws below stay inside these ranges and needn't reach their ends.
All inputs are finite; a program needn't handle non-finite values.
Results may differ from the reference program's by a relative error of at most 0.023.
Values may be sent and summed in bfloat16 or wider, within the bound.
No kernel may reach another device: no remote copies, remote signals or barrier semaphores. Data moves between devices by JAX's collectives and lax.ppermute only.
A program may use at most 128 MiB of HBM per device.

```python
import jax
import jax.numpy as jnp
from jax import lax

D = 1536
HEADS = 12
HD = 128
POS_DEV = 192
L = 3072
SEQS = 8
N_SEQ = 16


def draw_queries(key, part):
    key = jax.random.fold_in(key, 11)
    first_key = jax.random.fold_in(key, 0)
    drawn = jax.random.truncated_normal(first_key, -4.0, 4.0, (SEQS, L, HEADS * HD))
    return drawn.astype(jnp.bfloat16)


def draw_key_vectors(key, part):
    key = jax.random.fold_in(key, 23)
    first_key = jax.random.fold_in(key, 0)
    drawn = jax.random.truncated_normal(first_key, -4.0, 4.0, (SEQS, L, HEADS * HD))
    return drawn.astype(jnp.bfloat16)


def shard_levels(own_key, extent, cuts, smallest, largest):
    def one(axis_at, shards_of):
        heights = jax.random.uniform(jax.random.fold_in(jax.random.fold_in(own_key, 6), axis_at), (shards_of,), jnp.float32, smallest / len(cuts), largest / len(cuts))
        return jnp.repeat(jnp.exp(heights), extent[axis_at] // shards_of).reshape((-1,) + (1,) * (len(extent) - axis_at - 1))

    level = one(*cuts[0])
    for cut in cuts[1:]:
        level = level * one(*cut)
    return level


def noise(key, dims, spread, most, shards=(), held_as=jnp.bfloat16):
    gain = shard_levels(key, dims, shards, -0.22, 0.18) if shards else 1.0
    values = jax.random.normal(key, dims, jnp.float32) * spread * gain
    return jnp.minimum(jnp.maximum(values, -most), most).astype(held_as)


def setup_inputs(seed: int = 0) -> dict:
    keys = jax.random.split(jax.random.key(seed), 7)
    return {
        "queries": draw_queries(jax.random.fold_in(keys[6], 71), 0),
        "key_vectors": draw_key_vectors(jax.random.fold_in(keys[6], 71), 0),
        "value_vectors": noise(keys[2], (SEQS, L, HEADS * HD), 1.0, 6.0, ((0, 8), (1, 16), (2, 2))),
        "residual": noise(keys[3], (SEQS, L, D), 0.3, 2.0, ((0, 8), (1, 16), (2, 2))),
        "out_weight": noise(keys[4], (HEADS * HD, D), (HEADS * HD // 16) ** -0.5, 0.625, ((0, 2),)),
        "cotangent": noise(keys[5], (SEQS, L, D), 1.0, 6.0, ((0, 8), (1, 16), (2, 2))),
    }


def blocked_sum(left_rows, right_rows):
    left_f = left_rows.reshape(N_SEQ, POS_DEV, L).astype(jnp.float32)
    right_f = right_rows.reshape(N_SEQ, POS_DEV, HD).astype(jnp.float32)
    partial_sums = jnp.einsum("nqk,nqd->nkd", left_f, right_f)
    rounded = lax.optimization_barrier(partial_sums.astype(jnp.bfloat16))
    return jnp.sum(rounded.astype(jnp.float32), axis=0).astype(jnp.bfloat16)


def seq_pass(items):
    queries_s, keys_s, values_s, grads_s = items
    score_scale = HD ** -0.5
    attended_list, dq_list, dk_list, dv_list = [], [], [], []
    for head_idx in range(HEADS):
        columns = slice(head_idx * HD, (head_idx + 1) * HD)
        query_head = queries_s[:, columns]
        key_head = keys_s[:, columns]
        value_head = values_s[:, columns]
        grad_head = grads_s[:, columns]
        scores = jnp.dot(query_head, key_head.T, preferred_element_type=jnp.float32) * score_scale
        attn_prob = jax.nn.softmax(scores, axis=-1)
        prob_bf = attn_prob.astype(jnp.bfloat16)
        attended_list.append(jnp.dot(prob_bf, value_head, preferred_element_type=jnp.float32).astype(jnp.bfloat16))
        dprob = jnp.dot(grad_head, value_head.T, preferred_element_type=jnp.float32)
        row_delta = jnp.sum(attn_prob * dprob, axis=-1, keepdims=True)
        dscore = (attn_prob * (dprob - row_delta) * score_scale).astype(jnp.bfloat16)
        dq_list.append(jnp.dot(dscore, key_head, preferred_element_type=jnp.float32).astype(jnp.bfloat16))
        dk_list.append(blocked_sum(dscore, query_head))
        dv_list.append(blocked_sum(prob_bf, grad_head))
    return (jnp.concatenate(attended_list, axis=1), jnp.concatenate(dq_list, axis=1),
            jnp.concatenate(dk_list, axis=1), jnp.concatenate(dv_list, axis=1))


def reference(queries, key_vectors, value_vectors, residual, out_weight, cotangent):
    weight_float = out_weight.astype(jnp.float32)
    cotangent_float = cotangent.astype(jnp.float32)
    attention_gradient = jnp.einsum("vni,bi->vnb", cotangent_float, weight_float).astype(jnp.bfloat16)
    attended, grad_queries, grad_keys, grad_values = lax.map(
        seq_pass, (queries, key_vectors, value_vectors, attention_gradient))
    attended_float = attended.astype(jnp.float32)
    projected_output = jnp.einsum("qnf,fk->qnk", attended_float, weight_float)
    layer_out = (residual.astype(jnp.float32) + projected_output).astype(jnp.bfloat16)
    projection_weight_gradient = jnp.einsum("xuw,xua->wa", attended_float, cotangent_float)
    return layer_out, grad_queries, grad_keys, grad_values, projection_weight_gradient
```

```python
import jax
import jax.numpy as jnp
from jax import lax
from jax.experimental import pallas as pl
from jax.experimental.pallas import tpu as pltpu
from jax.sharding import Mesh
from jax.sharding import PartitionSpec as P

HD = 128
NY = 4
NZ = 8
SCALE = HD**-0.5
LOG2E = 1.4426950408889634
BF = jnp.bfloat16
F32 = jnp.float32
VMEM = 56 * 1024 * 1024


def shift(value, axis, step, size):
    return lax.ppermute(value, axis, [(i, (i + step) % size) for i in range(size)])


def swap(value, axis):
    return shift(value, axis, 1, 2)


def dot(a, b, ca, cb):
    return lax.dot_general(a, b, (((ca,), (cb,)), ((), ())), preferred_element_type=F32)


def keys_of(ref):
    return ref[0]


def values_of(ref):
    return ref[1]


def forward_kernel(n_kv, first, last, *refs):
    q0, q1 = refs[:2]
    kv = refs[2 : 2 + n_kv]
    at = 2 + n_kv
    query = jnp.concatenate([q0[...], q1[...]], axis=0)
    rows = query.shape[0]
    if first:
        top = jnp.full((1, rows), -jnp.inf, F32)
        total = jnp.zeros((1, rows), F32)
        acc = jnp.zeros((HD, rows), F32)
    else:
        top, total, acc = refs[at][0], refs[at + 1][0], refs[at + 2][0]
        at += 3
    factor = SCALE * LOG2E
    for ref in kv:
        scores = dot(keys_of(ref), query, 1, 1) * factor
        new_top = jnp.maximum(top, jnp.max(scores, axis=0, keepdims=True))
        decay = jnp.exp2(top - new_top)
        weight = jnp.exp2(scores - new_top)
        total = total * decay + jnp.sum(weight, axis=0, keepdims=True)
        acc = acc * decay + dot(values_of(ref), weight.astype(BF), 0, 0)
        top = new_top
    if last:
        out0, out1, level = refs[at : at + 3]
        attended = (acc / total).T.astype(BF)
        half = rows // 2
        out0[...] = attended[:half]
        out1[...] = attended[half:]
        level[0] = top + jnp.log2(total)
    else:
        refs[at][0] = top
        refs[at + 1][0] = total
        refs[at + 2][0] = acc


def head_block(rows, h0):
    return pl.BlockSpec((rows, HD), lambda h: (0, h0 + h))


def kv_block(rows, h0):
    return pl.BlockSpec((2, rows, HD), lambda h: (0, 0, h0 + h))


def stat_block(d1, d2, h0=0):
    return pl.BlockSpec((1, d1, d2), lambda h: (h0 + h, 0, 0))


def forward(q0, q1, kv, carry, last):
    rows, width = q0.shape
    heads = width // HD
    n_kv = len(kv)
    first = carry is None
    stat = jax.ShapeDtypeStruct((heads, 1, 2 * rows), F32)
    stat_spec = stat_block(1, 2 * rows)
    acc_spec = stat_block(HD, 2 * rows)
    carried = [] if first else list(carry)
    if last:
        out_shape = [jax.ShapeDtypeStruct((rows, width), BF)] * 2 + [stat]
        out_specs = [head_block(rows, 0)] * 2 + [stat_spec]
    else:
        out_shape = [stat, stat, jax.ShapeDtypeStruct((heads, HD, 2 * rows), F32)]
        out_specs = [stat_spec, stat_spec, acc_spec]
    cells = heads * 2 * rows * rows * n_kv
    return pl.pallas_call(
        lambda *refs: forward_kernel(n_kv, first, last, *refs),
        grid=(heads,),
        in_specs=[head_block(rows, 0)] * 2
        + [kv_block(rows, 0)] * n_kv
        + ([] if first else [stat_spec, stat_spec, acc_spec]),
        out_specs=out_specs,
        out_shape=out_shape,
        compiler_params=pltpu.CompilerParams(vmem_limit_bytes=VMEM),
        cost_estimate=pl.CostEstimate(
            flops=cells * HD * 4, bytes_accessed=n_kv * rows * width * 4, transcendentals=cells
        ),
    )(q0, q1, *kv, *carried)


def backward_kernel(n_own, n_kv, *refs):
    q0, q1, g0, g1, level_ref = refs[:5]
    kv = refs[5 : 5 + n_kv]
    dq0, dq1 = refs[5 + n_kv : 7 + n_kv]
    own = refs[7 + n_kv : 7 + n_kv + n_own]
    other, prob_buf, dprob_buf = refs[7 + n_kv + n_own :]
    query = jnp.concatenate([q0[...], q1[...]], axis=0)
    grad = jnp.concatenate([g0[...], g1[...]], axis=0)
    rows = query.shape[0]
    half = rows // 2
    level = level_ref[0]
    factor = SCALE * LOG2E
    delta = jnp.zeros((1, rows), F32)

    def place(i, which, value):
        r, x, c = i // 4, (i // 2) % 2, i % 2
        if c == 0:
            own[r][x, which] = value
        else:
            other[r, x, which] = value

    for i, ref in enumerate(kv):
        scores = dot(keys_of(ref), query, 1, 1) * factor
        prob = jnp.exp2(scores - level)
        dprob = dot(values_of(ref), grad, 1, 1)
        delta = delta + jnp.sum(prob * dprob, axis=0, keepdims=True)
        prob_buf[i] = prob
        dprob_buf[i] = dprob
        place(i, 1, dot(prob.astype(BF), grad, 1, 0).astype(BF))
    dq = jnp.zeros((HD, rows), F32)
    for i, ref in enumerate(kv):
        dscore = (prob_buf[i] * (dprob_buf[i] - delta)).astype(BF)
        place(i, 0, (dot(dscore, query, 1, 0) * SCALE).astype(BF))
        dq = dq + dot(keys_of(ref), dscore, 0, 0)
    dq_rows = (dq * SCALE).T.astype(BF)
    dq0[...] = dq_rows[:half]
    dq1[...] = dq_rows[half:]


def backward(q0, q1, g0, g1, level, kv, h0, heads):
    rows = q0.shape[0]
    n_kv = len(kv)
    width = heads * HD
    cells = heads * 2 * rows * rows * n_kv
    own_shape = jax.ShapeDtypeStruct((2, 2, rows, width), BF)
    own_spec = pl.BlockSpec((2, 2, rows, HD), lambda h: (0, 0, 0, h))
    return pl.pallas_call(
        lambda *refs: backward_kernel(NY, n_kv, *refs),
        grid=(heads,),
        in_specs=[head_block(rows, h0)] * 4
        + [stat_block(1, 2 * rows, h0)]
        + [kv_block(rows, h0)] * n_kv,
        out_specs=[head_block(rows, 0)] * 2
        + [own_spec] * NY
        + [pl.BlockSpec((NY, 2, 2, rows, HD), lambda h: (0, 0, 0, 0, h))],
        out_shape=[jax.ShapeDtypeStruct((rows, width), BF)] * 2
        + [own_shape] * NY
        + [jax.ShapeDtypeStruct((NY, 2, 2, rows, width), BF)],
        scratch_shapes=[pltpu.VMEM((n_kv, rows, 2 * rows), F32)] * 2,
        compiler_params=pltpu.CompilerParams(vmem_limit_bytes=VMEM),
        cost_estimate=pl.CostEstimate(
            flops=cells * HD * 10, bytes_accessed=n_kv * rows * width * 8, transcendentals=cells
        ),
    )(q0, q1, g0, g1, level, *kv)


def by_x(x, mine, theirs, axis):
    return jnp.where(
        x == 0,
        jnp.concatenate([mine, theirs], axis=axis),
        jnp.concatenate([theirs, mine], axis=axis),
    )


def body(queries, key_vectors, value_vectors, residual, out_weight, cotangent):
    x = lax.axis_index("x")
    y = lax.axis_index("y")
    c = lax.axis_index("c")
    t = lax.axis_index("tile")
    rows = queries.shape[1]
    width = queries.shape[2]
    group = width // 2

    def columns(value, which):
        return lax.dynamic_slice_in_dim(value, which * group, group, value.ndim - 1)

    kv_local = jnp.stack([key_vectors[0], value_vectors[0]])
    kv_mine = columns(kv_local, x)
    kv_theirs = columns(kv_local, 1 - x)
    kv_got = swap(kv_theirs, "x")
    cot_other = swap(cotangent[0], "tile")
    query_mine = columns(queries[0], x)
    query_got = swap(columns(queries[0], 1 - x), "x")

    def all_y(value):
        return [value] + [shift(value, "y", r, NY) for r in range(1, NY)]

    set_mine = all_y(kv_mine)
    set_got = all_y(kv_got)
    pair_mine = [(v, swap(v, "c")) for v in set_mine]
    pair_got = [(v, swap(v, "c")) for v in set_got]

    cot_full = by_x(t, cotangent[0], cot_other, 1)
    attention_gradient = dot(cot_full, out_weight, 1, 1).astype(BF)
    grad_mine = columns(attention_gradient, x)
    grad_got = swap(columns(attention_gradient, 1 - x), "x")
    cot_got = swap(cot_full, "x")

    carry = forward(query_mine, query_got, [v for p in pair_mine for v in p], None, False)
    out_mine, out_got, level = forward(
        query_mine, query_got, [v for p in pair_got for v in p], carry, True
    )

    partial = dot(out_mine, cot_full, 0, 0) + dot(out_got, cot_got, 0, 0)
    half = group // 2
    part_keep = lax.dynamic_slice_in_dim(partial, c * half, half, 0)
    part_send = lax.dynamic_slice_in_dim(partial, (1 - c) * half, half, 0).astype(BF)
    part = (part_keep + swap(part_send, "c").astype(F32)).astype(BF)
    model = part.shape[1]
    span = model // NY

    def span_of(which):
        return lax.dynamic_slice_in_dim(part, lax.rem(which + NY, NY) * span, span, 1)

    own_span = span_of(y).astype(F32)
    for r in range(1, NY):
        own_span = own_span + shift(span_of(y + r), "y", r, NY).astype(F32)
    pieces = lax.all_to_all(own_span.astype(BF).reshape(NZ, half // NZ, span), "dp", 0, 0)
    piece = jnp.sum(pieces.astype(F32), axis=0).astype(BF)
    whole = lax.all_gather(piece, "dp", axis=0, tiled=True)
    both = jnp.stack([whole, swap(whole, "x")])
    spans = all_y(both)
    weight_pairs = [(v, swap(v, "c")) for v in spans]
    out = jnp.zeros((width, model), F32)
    for r, pair in enumerate(weight_pairs):
        column = lax.rem(y - r + NY, NY) * span
        for cr, value in enumerate(pair):
            for xr in range(2):
                row = (x + xr) % 2 * group + (c + cr) % 2 * half
                out = lax.dynamic_update_slice(out, value[xr].astype(F32), (row, column))
    weight_gradient = out

    attended = by_x(x, out_mine, swap(out_got, "x"), 1)
    projected = dot(attended, out_weight, 1, 0)
    keep = lax.dynamic_slice_in_dim(projected, t * width, width, 1)
    send = lax.dynamic_slice_in_dim(projected, (1 - t) * width, width, 1).astype(BF)
    layer_out = (
        residual[0].astype(F32) + keep + swap(send, "tile").astype(F32)
    ).astype(BF)

    kv_all = []
    for r in range(NY):
        kv_all += list(pair_mine[r]) + list(pair_got[r])
    grads = []
    dqs = []
    for h0, heads in ((0, 2), (2, 1)):
        res = backward(query_mine, query_got, grad_mine, grad_got, level, kv_all, h0, heads)
        dq_mine, dq_got = res[:2]
        own, other = res[2 : 2 + NY], res[2 + NY]
        arrived = swap(other, "c")
        sums = [own[r].astype(F32) + arrived[r].astype(F32) for r in range(NY)]
        total = sums[0]
        for r in range(1, NY):
            total = total + shift(sums[r].astype(BF), "y", -r, NY).astype(F32)
        total = total.astype(BF)
        grads.append((total[0], swap(total[1], "x")))
        dqs.append((dq_mine, swap(dq_got, "x")))

    def joined(index, pick):
        return jnp.concatenate([pick(g[index]) for g in grads], axis=-1)

    def assemble(pick):
        return by_x(x, joined(0, pick), joined(1, pick), 1)

    grad_keys = assemble(lambda v: v[0])
    grad_values = assemble(lambda v: v[1])
    grad_queries = by_x(
        x,
        jnp.concatenate([d[0] for d in dqs], axis=1),
        jnp.concatenate([d[1] for d in dqs], axis=1),
        1,
    )
    return (layer_out[None], grad_queries[None], grad_keys[None], grad_values[None], weight_gradient)


def solution(mesh):
    fine = Mesh(mesh.devices.reshape(NZ, NY, 2, 2, 2), ("dp", "y", "x", "c", "tile"))
    rows = P("dp", ("y", "x", "c"), "tile")
    return jax.shard_map(
        body,
        mesh=fine,
        in_specs=(rows, rows, rows, rows, P("tile", None), rows),
        out_specs=(rows, rows, rows, rows, P("tile", None)),
        check_vma=False,
    )
```

```python
import jax
import jax.numpy as jnp
from jax import lax
from jax.experimental import pallas as pl
from jax.experimental.pallas import tpu as pltpu
from jax.sharding import Mesh
from jax.sharding import PartitionSpec as P

HD = 128
NY = 4
NZ = 8
ORDER = (1, 3, 2)
SCALE = HD**-0.5
LOG2E = 1.4426950408889634
BF = jnp.bfloat16
F32 = jnp.float32
COST = pl.CostEstimate(flops=1, bytes_accessed=1, transcendentals=0)
VMEM = 56 * 1024 * 1024


def shift(value, axis, step, size):
    return lax.ppermute(value, axis, [(i, (i + step) % size) for i in range(size)])


def swap(value, axis):
    return shift(value, axis, 1, 2)


def hold(*values):
    return lax.optimization_barrier(values)


def dot(a, b, ca, cb):
    return lax.dot_general(a, b, (((ca,), (cb,)), ((), ())), preferred_element_type=F32)


PLACES = [(r, x, c) for c in range(2) for r in range(4) for x in range(2) if (r, x) != (3, 1)]
PLACES += [(3, 1, 0), (3, 1, 1)]


def blocks_of(refs):
    blocks = []
    for ref in refs:
        if len(ref.shape) == 4:
            blocks += [(ref, (r,)) for r in range(ref.shape[0])]
        else:
            blocks.append((ref, ()))
    return blocks


def keys_of(block):
    return block[0][(*block[1], 0)]


def values_of(block):
    return block[0][(*block[1], 1)]


def groups_of(count):
    return [(i, min(i + 4, count)) for i in range(0, count, 4)]


def merged(blocks):
    return jnp.concatenate(blocks, axis=0)


def forward_kernel(n_arrays, first, last, *refs):
    q0, q1 = refs[:2]
    kv = blocks_of(refs[2 : 2 + n_arrays])
    n_kv = len(kv)
    at = 2 + n_arrays
    scores_buf = refs[-1]
    query = jnp.concatenate([q0[...], q1[...]], axis=0)
    rows = query.shape[0]
    if first:
        top = jnp.full((1, rows), -jnp.inf, F32)
    else:
        top, total, acc = refs[at][0], refs[at + 1][0], refs[at + 2][0]
        at += 3
    factor = SCALE * LOG2E
    new_top = top
    for i, ref in enumerate(kv):
        scores = dot(keys_of(ref), query, 1, 1) * factor
        scores_buf[i] = scores
        new_top = jnp.maximum(new_top, jnp.max(scores, axis=0, keepdims=True))
    if first:
        total = jnp.zeros((1, rows), F32)
        acc = jnp.zeros((HD, rows), F32)
    else:
        decay = jnp.exp2(top - new_top)
        total = total * decay
        acc = acc * decay
    top = new_top
    for i, end in groups_of(n_kv):
        weight = jnp.exp2(scores_buf[i:end] - top[None])
        total = total + jnp.sum(weight, axis=(0, 1))[None]
        weight = weight.astype(BF).reshape(-1, rows)
        acc = acc + dot(merged([values_of(ref) for ref in kv[i:end]]), weight, 0, 0)
    if last:
        out, level = refs[at : at + 2]
        out[...] = (acc / total).T.astype(BF)
        level[0] = top + jnp.log2(total)
    else:
        refs[at][0] = top
        refs[at + 1][0] = total
        refs[at + 2][0] = acc


def head_block(rows, h0):
    return pl.BlockSpec((rows, HD), lambda h: (0, h0 + h))


def kv_block(value, h0):
    lead = value.shape[:-1]
    return pl.BlockSpec((*lead, HD), lambda h: (0,) * len(lead) + (h0 + h,))


def stat_block(d1, d2, h0=0):
    return pl.BlockSpec((1, d1, d2), lambda h: (h0 + h, 0, 0))


def forward(q0, q1, kv, carry, last):
    rows, width = q0.shape
    heads = width // HD
    n_arrays = len(kv)
    n_kv = sum(v.shape[0] if v.ndim == 4 else 1 for v in kv)
    first = carry is None
    stat = jax.ShapeDtypeStruct((heads, 1, 2 * rows), F32)
    stat_spec = stat_block(1, 2 * rows)
    acc_spec = stat_block(HD, 2 * rows)
    carried = [] if first else list(carry)
    if last:
        out_shape = [jax.ShapeDtypeStruct((2 * rows, width), BF), stat]
        out_specs = [head_block(2 * rows, 0), stat_spec]
    else:
        out_shape = [stat, stat, jax.ShapeDtypeStruct((heads, HD, 2 * rows), F32)]
        out_specs = [stat_spec, stat_spec, acc_spec]
    return pl.pallas_call(
        lambda *refs: forward_kernel(n_arrays, first, last, *refs),
        grid=(heads,),
        in_specs=[head_block(rows, 0)] * 2
        + [kv_block(v, 0) for v in kv]
        + ([] if first else [stat_spec, stat_spec, acc_spec]),
        out_specs=out_specs,
        out_shape=out_shape,
        scratch_shapes=[pltpu.VMEM((n_kv, rows, 2 * rows), F32)],
        compiler_params=pltpu.CompilerParams(vmem_limit_bytes=VMEM),
        cost_estimate=COST,
    )(q0, q1, *kv, *carried)


def split_kernel(x_ref, q, k, v, q_mine, q_theirs, kv_mine, kv_theirs):
    group = q_mine.shape[1]
    mine = pl.ds(pl.multiple_of(x_ref[0] * group, HD), group)
    theirs = pl.ds(pl.multiple_of((1 - x_ref[0]) * group, HD), group)
    q_mine[...] = q[:, mine]
    q_theirs[...] = q[:, theirs]
    kv_mine[0] = k[:, mine]
    kv_mine[1] = v[:, mine]
    kv_theirs[0] = k[:, theirs]
    kv_theirs[1] = v[:, theirs]


def split_heads(x, q, k, v):
    rows, width = q.shape
    one = jax.ShapeDtypeStruct((rows, width // 2), BF)
    two = jax.ShapeDtypeStruct((2, rows, width // 2), BF)
    whole = pl.BlockSpec(memory_space=pltpu.VMEM)
    return pl.pallas_call(
        split_kernel,
        in_specs=[pl.BlockSpec(memory_space=pltpu.SMEM)] + [whole] * 3,
        out_specs=[whole] * 4,
        out_shape=[one, one, two, two],
        compiler_params=pltpu.CompilerParams(vmem_limit_bytes=VMEM),
    )(x.reshape(1).astype(jnp.int32), q, k, v)


def backward_kernel(n_arrays, *refs):
    q0, q1, g0, g1, level_ref = refs[:5]
    kv = blocks_of(refs[5 : 5 + n_arrays])
    dq0, dq1 = refs[5 + n_arrays : 7 + n_arrays]
    own = refs[7 + n_arrays : 7 + n_arrays + NY]
    other, prob_buf, dprob_buf = refs[7 + n_arrays + NY :]
    query = jnp.concatenate([q0[...], q1[...]], axis=0)
    grad = jnp.concatenate([g0[...], g1[...]], axis=0)
    rows = query.shape[0]
    half = rows // 2
    level = level_ref[0]
    factor = SCALE * LOG2E
    delta = jnp.zeros((1, rows), F32)

    def place(i, which, value):
        r, x, c = PLACES[i]
        if c == 0:
            own[r][x, which] = value
        else:
            other[r, x, which] = value

    for i, ref in enumerate(kv):
        scores = dot(keys_of(ref), query, 1, 1) * factor
        prob = jnp.exp2(scores - level)
        dprob = dot(values_of(ref), grad, 1, 1)
        delta = delta + jnp.sum(prob * dprob, axis=0, keepdims=True)
        prob_buf[i] = prob
        dprob_buf[i] = dprob
        place(i, 1, dot(prob.astype(BF), grad, 1, 0).astype(BF))
    dq = jnp.zeros((HD, rows), F32)
    for i, end in groups_of(len(kv)):
        dscore = (prob_buf[i:end] * (dprob_buf[i:end] - delta[None])).astype(BF)
        for j in range(end - i):
            place(i + j, 0, (dot(dscore[j], query, 1, 0) * SCALE).astype(BF))
        dq = dq + dot(
            merged([keys_of(ref) for ref in kv[i:end]]), dscore.reshape(-1, rows), 0, 0
        )
    dq_rows = (dq * SCALE).T.astype(BF)
    dq0[...] = dq_rows[:half]
    dq1[...] = dq_rows[half:]


def backward(q0, q1, g0, g1, level, kv, h0, heads):
    rows = q0.shape[0]
    n_kv = 4 * NY
    width = heads * HD
    own_shape = jax.ShapeDtypeStruct((2, 2, rows, width), BF)
    own_spec = pl.BlockSpec((2, 2, rows, HD), lambda h: (0, 0, 0, h))
    return pl.pallas_call(
        lambda *refs: backward_kernel(len(kv), *refs),
        grid=(heads,),
        in_specs=[head_block(rows, h0)] * 4
        + [stat_block(1, 2 * rows, h0)]
        + [kv_block(v, h0) for v in kv],
        out_specs=[head_block(rows, 0)] * 2
        + [own_spec] * NY
        + [pl.BlockSpec((NY, 2, 2, rows, HD), lambda h: (0, 0, 0, 0, h))],
        out_shape=[jax.ShapeDtypeStruct((rows, width), BF)] * 2
        + [own_shape] * NY
        + [jax.ShapeDtypeStruct((NY, 2, 2, rows, width), BF)],
        scratch_shapes=[pltpu.VMEM((n_kv, rows, 2 * rows), F32)] * 2,
        compiler_params=pltpu.CompilerParams(vmem_limit_bytes=VMEM),
        cost_estimate=COST,
    )(q0, q1, g0, g1, level, *kv)


def by_x(x, mine, theirs, axis):
    return jnp.where(
        x == 0,
        jnp.concatenate([mine, theirs], axis=axis),
        jnp.concatenate([theirs, mine], axis=axis),
    )


def body(queries, key_vectors, value_vectors, residual, out_weight, cotangent):
    x = lax.axis_index("x")
    y = lax.axis_index("y")
    c = lax.axis_index("c")
    t = lax.axis_index("tile")
    rows = queries.shape[1]
    width = queries.shape[2]
    group = width // 2

    def columns(value, which):
        return lax.dynamic_slice_in_dim(value, which * group, group, value.ndim - 1)

    query_mine, query_theirs, kv_mine, kv_theirs = split_heads(
        x, queries[0], key_vectors[0], value_vectors[0]
    )
    kv_got = swap(kv_theirs, "x")
    near_mine = [shift(kv_mine, "y", r, NY) for r in ORDER]
    cot_other = swap(cotangent[0], "tile")
    kv_got, query_theirs = hold(kv_got, query_theirs)
    near_got = [shift(kv_got, "y", r, NY) for r in ORDER[:2]]
    far_got = shift(kv_got, "y", ORDER[2], NY)
    query_got = swap(query_theirs, "x")

    cot_full = by_x(t, cotangent[0], cot_other, 1)
    attention_gradient = dot(cot_full, out_weight, 1, 1).astype(BF)
    grad_mine = columns(attention_gradient, x)
    grad_theirs = columns(attention_gradient, 1 - x)
    cot_got = swap(cot_full, "x")

    near_mine, near_got, grad_theirs, query_got = hold(
        near_mine, near_got, grad_theirs, query_got
    )
    near = [kv_mine, kv_got]
    for pair in zip(near_mine, near_got):
        near += pair
    near.append(near_mine[2])
    near.append(swap(jnp.stack(near), "c"))
    carry = forward(query_mine, query_got, near, None, False)
    carry, far_got, cot_got = hold(carry, far_got, cot_got)
    grad_got = swap(grad_theirs, "x")
    model = cot_full.shape[1]
    half = model // 2

    def model_half(core):
        return jnp.concatenate(
            [lax.dynamic_slice_in_dim(v, core * half, half, 1) for v in (cot_full, cot_got)]
        )

    cot_keep, cot_send = model_half(c), model_half(1 - c)
    far = [far_got, swap(far_got, "c")]
    far, cot_keep, cot_send = hold(far, cot_keep, cot_send)
    out, level = forward(query_mine, query_got, far, carry, True)
    out, grad_got = hold(out, grad_got)
    out_mine, out_got = out[:rows], out[rows:]

    part_got = swap(dot(out, cot_send, 0, 0).astype(BF), "c")
    part = (dot(out, cot_keep, 0, 0) + part_got.astype(F32)).astype(BF)
    span = group // NY
    spans_out = [
        lax.dynamic_slice_in_dim(part, lax.rem(y + r, NY) * span, span, 0) for r in (0, *ORDER)
    ]

    kv_all = near + far

    def backward_heads(query, h0, heads):
        return backward(query, query_got, grad_mine, grad_got, level, kv_all, h0, heads)

    def chip_sums(res, arrived):
        own = res[2 : 2 + NY]
        first = own[0].astype(F32) + arrived[0].astype(F32)
        return [first] + [
            (own[r].astype(F32) + arrived[r].astype(F32)).astype(BF) for r in range(1, NY)
        ]

    def to_owners(sums):
        return [shift(value, "y", -r, NY) for value, r in zip(sums[1:], ORDER)]

    def total_of(first, others):
        total = first.astype(F32)
        for value in others:
            total = total + value.astype(F32)
        return total.astype(BF)

    def from_z(value, bit):
        return lax.ppermute(value, "dp", [(i, i ^ bit) for i in range(NZ)])

    def returned(sums, owned, res):
        total = total_of(sums[0], owned)
        kept = jnp.concatenate([total[0], res[0][None]])
        return kept, swap(jnp.concatenate([total[1], res[1][None]]), "x")

    spans_out, query_a, out_got = hold(spans_out, query_mine, out_got)
    spans_in = [shift(v, "y", r, NY) for v, r in zip(spans_out[1:], ORDER)]
    out_back = swap(out_got, "x")
    res_a = backward_heads(query_a, 0, 2)
    res_a, spans_in, out_back = hold(res_a, spans_in, out_back)

    z0, out_mine = hold(total_of(spans_out[0], spans_in), out_mine)
    z0_in = from_z(z0, 1)
    sums_a = chip_sums(res_a, swap(res_a[2 + NY], "c"))
    attended = by_x(x, out_mine, out_back, 1)
    projected = dot(attended, out_weight, 1, 0)
    keep = lax.dynamic_slice_in_dim(projected, t * width, width, 1)
    send = lax.dynamic_slice_in_dim(projected, (1 - t) * width, width, 1).astype(BF)
    z0_in, send, sums_a = hold(z0_in, send, sums_a)

    owned_a = to_owners(sums_a)
    z1, query_b = hold(total_of(z0, [z0_in]), query_mine)
    z1_in = from_z(z1, 2)
    res_b = backward_heads(query_b, 2, 1)
    res_b, z1_in, owned_a[0], owned_a[1] = hold(res_b, z1_in, owned_a[0], owned_a[1])

    z2 = total_of(z1, [z1_in])
    z2_in = from_z(z2, 4)
    sums_b = chip_sums(res_b, swap(res_b[2 + NY], "c"))
    sent_back = swap(send, "tile")
    z2_in, sums_b, owned_a[2] = hold(z2_in, sums_b, owned_a[2])

    z4 = total_of(z2, [z2_in])
    spans_back = [shift(z4, "y", r, NY) for r in ORDER]
    kept_a, back_a = returned(sums_a, owned_a, res_a)
    owned_b = to_owners(sums_b)
    spans_back, back_a, sent_back = hold(spans_back, back_a, sent_back)
    spans = jnp.stack([z4, *spans_back])
    spans_got, owned_b = hold(swap(spans, "x"), owned_b)
    ours = jnp.stack([spans, spans_got])
    weight_gradient = jnp.zeros((width, model), F32)
    for cr, block in enumerate((ours, swap(ours, "c"))):
        column = (c + cr) % 2 * half
        for i, r in enumerate((0, *ORDER)):
            for xr in range(2):
                row = (x + xr) % 2 * group + lax.rem(y - r + NY, NY) * span
                weight_gradient = lax.dynamic_update_slice(
                    weight_gradient, block[xr, i].astype(F32), (row, column)
                )
    layer_out = (residual[0].astype(F32) + keep + sent_back.astype(F32)).astype(BF)

    kept_b, back_b = returned(sums_b, owned_b, res_b)
    grads = by_x(
        x, jnp.concatenate([kept_a, kept_b], axis=2), jnp.concatenate([back_a, back_b], axis=2), 2
    )
    return (layer_out[None], grads[2][None], grads[0][None], grads[1][None], weight_gradient)


def solution(mesh):
    fine = Mesh(mesh.devices.reshape(NZ, NY, 2, 2, 2), ("dp", "y", "x", "c", "tile"))
    rows = P("dp", ("y", "x", "c"), "tile")
    return jax.shard_map(
        body,
        mesh=fine,
        in_specs=(rows, rows, rows, rows, P("tile", None), rows),
        out_specs=(rows, rows, rows, rows, P("tile", None)),
        check_vma=False,
    )
```

```python
import jax
import jax.numpy as jnp
from jax import lax
from jax.experimental import pallas as pl
from jax.experimental.pallas import tpu as pltpu
from jax.sharding import Mesh
from jax.sharding import PartitionSpec as P

HD = 128
NY = 4
NZ = 8
ORDER = (1, 3, 2)
SCALE = HD**-0.5
LOG2E = 1.4426950408889634
FACTOR = SCALE * LOG2E
BF = jnp.bfloat16
F32 = jnp.float32
COST = pl.CostEstimate(flops=1, bytes_accessed=1, transcendentals=0)
PARAMS = pltpu.CompilerParams(vmem_limit_bytes=56 * 1024 * 1024)
IN_VMEM = pl.BlockSpec(memory_space=pltpu.VMEM)
IN_SMEM = pl.BlockSpec(memory_space=pltpu.SMEM)
RUN = 4
STATS = 8


def shift(value, axis, step, size):
    return lax.ppermute(value, axis, [(i, (i + step) % size) for i in range(size)])


def swap(value, axis):
    return shift(value, axis, 1, 2)


def hold(*values):
    return lax.optimization_barrier(values)


def dot(a, b, ca, cb):
    return lax.dot_general(a, b, (((ca,), (cb,)), ((), ())), preferred_element_type=F32)


def shaped(*shape, dtype=BF):
    return jax.ShapeDtypeStruct(shape, dtype)


def call(kernel, scalars, arrays, out_shape, scratch_shapes=()):
    return pl.pallas_call(
        kernel,
        in_specs=[IN_SMEM] * len(scalars) + [IN_VMEM] * len(arrays),
        out_specs=[IN_VMEM] * len(out_shape),
        out_shape=out_shape,
        scratch_shapes=list(scratch_shapes),
        compiler_params=PARAMS,
        cost_estimate=COST,
    )(*[s.reshape(1).astype(jnp.int32) for s in scalars], *arrays)


def split_kernel(x_ref, q, k, v, q_mine, q_theirs, kv_mine, kv_theirs):
    group = q_mine.shape[1]
    mine = pl.ds(pl.multiple_of(x_ref[0] * group, HD), group)
    theirs = pl.ds(pl.multiple_of((1 - x_ref[0]) * group, HD), group)
    kv_theirs[0] = k[:, theirs]
    kv_theirs[1] = v[:, theirs]
    kv_mine[0] = k[:, mine]
    kv_mine[1] = v[:, mine]
    q_mine[...] = q[:, mine]
    q_theirs[...] = q[:, theirs]


def split_heads(x, q, k, v):
    rows, width = q.shape
    one = shaped(rows, width // 2)
    two = shaped(2, rows, width // 2)
    return call(split_kernel, [x], [q, k, v], [one, one, two, two])


def head_columns(h):
    return slice(h * HD, (h + 1) * HD)


def stacked(refs, h):
    return jnp.concatenate([ref[:, head_columns(h)] for ref in refs], axis=0)


def run_of(refs, which, h):
    return jnp.concatenate([ref[which, :, head_columns(h)] for ref in refs], axis=0)


def runs(kv):
    return [kv[i : i + RUN] for i in range(0, len(kv), RUN)]


def softmax_over(kv, h, query, scores_buf):
    columns = query.shape[0]
    top = jnp.full((1, columns), -jnp.inf, F32)
    for i, refs in enumerate(runs(kv)):
        scores = dot(run_of(refs, 0, h), query, 1, 1) * FACTOR
        scores_buf[h % 2, i] = scores
        top = jnp.maximum(top, jnp.max(scores, axis=0, keepdims=True))
    total = jnp.zeros((1, columns), F32)
    acc = jnp.zeros((HD, columns), F32)
    for i, refs in enumerate(runs(kv)):
        weight = jnp.exp2(scores_buf[h % 2, i] - top)
        total = total + jnp.sum(weight, axis=0, keepdims=True)
        acc = acc + dot(run_of(refs, 1, h), weight.astype(BF), 0, 0)
    return top, total, acc


def forward_kernel(n_kv, heads, q0, q1, q2, q3, *refs):
    kv = refs[:n_kv]
    own, other, scores_buf = refs[n_kv:]
    columns = 2 * q0.shape[0]
    for h in range(heads):
        top, total, acc = softmax_over(kv, h, stacked((q0, q1, q2, q3), h), scores_buf)
        pad = jnp.zeros((STATS - 2, 2 * columns), F32)
        stats = jnp.concatenate([top, total, pad], axis=0)
        for out, part in ((own, slice(0, columns)), (other, slice(columns, 2 * columns))):
            out[h, :HD] = acc[:, part]
            out[h, HD:] = stats[:, part]


def merge_kernel(heads, own_ref, mine, got, g0, g1, cot0, cot1, tile0, tile1, *outs):
    out0, out1, stats, keep, send = outs
    rows = g0.shape[0]
    own = jnp.concatenate([cot0[...], cot1[...]], axis=0)
    tiles = jnp.concatenate([tile0[...], tile1[...]], axis=0)
    cot_keep = jnp.where(own_ref[0] == 1, own, tiles)
    cot_send = jnp.where(own_ref[0] == 1, tiles, own)
    for h in range(heads):
        top_a, total_a = mine[h, HD : HD + 1], mine[h, HD + 1 : HD + 2]
        top_b, total_b = got[h, HD : HD + 1], got[h, HD + 1 : HD + 2]
        top = jnp.maximum(top_a, top_b)
        scale_a, scale_b = jnp.exp2(top_a - top), jnp.exp2(top_b - top)
        total = total_a * scale_a + total_b * scale_b
        attended = (mine[h, :HD] * scale_a + got[h, :HD] * scale_b) / total
        delta = jnp.sum(
            attended * stacked((g0, g1), h).astype(F32).T, axis=0, keepdims=True
        )
        level = top + jnp.log2(total)
        pad = jnp.zeros((STATS - 2, 2 * rows), F32)
        stats[h] = jnp.concatenate([level, delta, pad], axis=0)
        rounded = attended.astype(BF)
        send[head_columns(h)] = dot(rounded, cot_send, 1, 0).astype(BF)
        keep[head_columns(h)] = dot(rounded, cot_keep, 1, 0)
        by_row = attended.T.astype(BF)
        out0[:, head_columns(h)] = by_row[:rows]
        out1[:, head_columns(h)] = by_row[rows:]


def forward(queries, kv):
    rows, width = queries[0].shape
    heads = width // HD
    return call(
        lambda *refs: forward_kernel(len(kv), heads, *refs),
        [],
        [*queries, *kv],
        [shaped(heads, HD + STATS, 2 * rows, dtype=F32)] * 2,
        [pltpu.VMEM((2, len(runs(kv)), RUN * rows, 4 * rows), F32)],
    )


def merge(own, mine, got, grads, cots):
    rows, width = grads[0].shape
    heads = width // HD
    half = cots[0].shape[1]
    return call(
        lambda *refs: merge_kernel(heads, *refs),
        [own],
        [mine, got, *grads, *cots],
        [
            shaped(rows, width),
            shaped(rows, width),
            shaped(heads, STATS, 2 * rows, dtype=F32),
            shaped(width, half, dtype=F32),
            shaped(width, half),
        ],
    )


def backward_kernel(heads, first, *refs):
    queries, grads, (stats_a, stats_b), kv = refs[:4], refs[4:8], refs[8:10], refs[10 : 10 + RUN]
    outs = refs[10 + RUN + (not first) :]
    rows = queries[0].shape[0]
    for h in range(heads):
        columns = head_columns(h)
        query = stacked(queries, h)
        grad = stacked(grads, h)
        stats = jnp.concatenate([stats_a[h], stats_b[h]], axis=1)
        level, delta = stats[0:1], stats[1:2]
        keys = run_of(kv, 0, h)
        prob = jnp.exp2(dot(keys, query, 1, 1) * FACTOR - level)
        dv = dot(prob.astype(BF), grad, 1, 0).astype(BF)
        dscore = (prob * (dot(run_of(kv, 1, h), grad, 1, 1) - delta)).astype(BF)
        dk = (dot(dscore, query, 1, 0) * SCALE).astype(BF)
        dq = dot(keys, dscore, 0, 0)
        for j in range(RUN):
            block = slice(j * rows, (j + 1) * rows)
            outs[j][0, :, columns] = dk[block]
            outs[j][1, :, columns] = dv[block]
        if first:
            outs[RUN][h] = dq
        else:
            dq_rows = ((dq + refs[10 + RUN][h]) * SCALE).T
            outs[RUN][:, columns] = dq_rows[:rows]
            outs[RUN + 1][:, columns] = dq_rows[rows : 2 * rows]
            outs[RUN + 2][:, columns] = dq_rows[2 * rows :].astype(BF)


def backward(queries, grads, stats, kv, dq):
    rows, width = queries[0].shape
    heads = width // HD
    first = dq is None
    if first:
        dq_shapes = [shaped(heads, HD, 4 * rows, dtype=F32)]
    else:
        dq_shapes = [shaped(rows, width, dtype=F32)] * 2 + [shaped(2 * rows, width)]
    return call(
        lambda *refs: backward_kernel(heads, first, *refs),
        [],
        [*queries, *grads, *stats, *kv] + ([] if first else [dq]),
        [shaped(2, rows, width)] * RUN + dq_shapes,
    )


def by_x(x, mine, theirs, axis):
    return jnp.where(
        x == 0,
        jnp.concatenate([mine, theirs], axis=axis),
        jnp.concatenate([theirs, mine], axis=axis),
    )


def total_of(first, others):
    total = first.astype(F32)
    for value in others:
        total = total + value.astype(F32)
    return total.astype(BF)


def body(queries, key_vectors, value_vectors, residual, out_weight, cotangent):
    x = lax.axis_index("x")
    y = lax.axis_index("y")
    c = lax.axis_index("c")
    t = lax.axis_index("tile")
    width = queries.shape[2]
    group = width // 2

    query_mine, query_theirs, kv_mine, kv_theirs = split_heads(
        x, queries[0], key_vectors[0], value_vectors[0]
    )
    cot_own = cotangent[0]
    cot_own = cotangent[0]
    kv_got = swap(kv_theirs, "x")
    mine_in = [shift(kv_mine, "y", r, NY) for r in ORDER]
    cot_other = swap(cot_own, "tile")
    query_mine_c = swap(query_mine, "c")
    kv_got, query_theirs, cot_sent = hold(kv_got, query_theirs, cot_own)
    got_in = [shift(kv_got, "y", r, NY) for r in ORDER]
    query_got = swap(query_theirs, "x")
    query_got_c = swap(query_got, "c")
    cot_own_got = swap(cot_sent, "x")

    def weight_columns(which):
        return lax.dynamic_slice_in_dim(out_weight, which * width, width, 1)

    attention_gradient = (
        dot(cot_own, weight_columns(t), 1, 1) + dot(cot_other, weight_columns(1 - t), 1, 1)
    ).astype(BF)
    grad_mine = lax.dynamic_slice_in_dim(attention_gradient, x * group, group, 1)
    grad_theirs = lax.dynamic_slice_in_dim(attention_gradient, (1 - x) * group, group, 1)
    grad_got = swap(grad_theirs, "x")
    cot_other_got = swap(cot_other, "x")
    mine_in, got_in, query_mine_c, query_got_c, grad_theirs = hold(
        mine_in, got_in, query_mine_c, query_got_c, grad_theirs
    )
    queries_all = [query_mine, query_got, query_mine_c, query_got_c]
    mine, others = forward(queries_all, [kv_mine, *mine_in, kv_got, *got_in])
    grad_mine_c = swap(grad_mine, "c")
    mine, others, grad_got, cot_own_got, cot_other_got, grad_mine_c = hold(
        mine, others, grad_got, cot_own_got, cot_other_got, grad_mine_c
    )
    merged = swap(others, "c")
    grad_got_c = swap(grad_got, "c")
    merged, grad_got_c = hold(merged, grad_got_c)
    out_mine, out_got, stats, keep, send = hold(
        *merge(
            c == t,
            mine,
            merged,
            [grad_mine, grad_got],
            [cot_own, cot_own_got, cot_other, cot_other_got],
        )
    )

    stats_c = swap(stats, "c")
    part = (keep + swap(send, "c").astype(F32)).astype(BF)
    span = group // NY
    spans_out = [
        lax.dynamic_slice_in_dim(part, lax.rem(y + r, NY) * span, span, 0) for r in (0, *ORDER)
    ]

    def to_owner(blocks, i):
        return shift(blocks[i + 1], "y", -ORDER[i], NY)

    def from_z(value, bit):
        return lax.ppermute(value, "dp", [(i, i ^ bit) for i in range(NZ)])

    spans_out, stats_c, out_got, query_mine = hold(spans_out, stats_c, out_got, query_mine)
    spans_in = [shift(v, "y", r, NY) for v, r in zip(spans_out[1:], ORDER)]
    out_back = swap(out_got, "x")
    grads_all = [grad_mine, grad_got, grad_mine_c, grad_got_c]
    rest = (grads_all, [stats, stats_c])
    got_grads = backward([query_mine, *queries_all[1:]], *rest, [kv_got, *got_in], None)
    got_grads, spans_in, out_back = hold(got_grads, spans_in, out_back)

    z0, query_mine = hold(total_of(spans_out[0], spans_in), query_mine)
    z0_in = from_z(z0, 1)
    owned_got = [to_owner(got_grads, i) for i in range(2)]
    mine_grads = backward(
        [query_mine, *queries_all[1:]], *rest, [kv_mine, *mine_in], got_grads[RUN]
    )
    mine_grads, z0_in, out_mine = hold(mine_grads, z0_in, out_mine)
    dq_mine, dq_got, dq_other = mine_grads[RUN:]

    z1, out_mine, dq_other = hold(total_of(z0, [z0_in]), out_mine, dq_other)
    z1_in = from_z(z1, 2)
    owned_got.append(to_owner(got_grads, 2))
    dq_other = swap(dq_other, "c").astype(F32)
    rows = dq_mine.shape[0]
    attended = by_x(x, out_mine, out_back, 1)
    projected = dot(attended, out_weight, 1, 0)
    kept = lax.dynamic_slice_in_dim(projected, t * width, width, 1)
    leaving = lax.dynamic_slice_in_dim(projected, (1 - t) * width, width, 1).astype(BF)
    dq_got = (dq_got + dq_other[rows:]).astype(BF)
    z1_in, leaving, owned_got[0], owned_got[1], dq_got = hold(
        z1_in, leaving, owned_got[0], owned_got[1], dq_got
    )

    z2 = total_of(z1, [z1_in])
    z2_in = from_z(z2, 4)
    arriving = swap(leaving, "tile")
    owned_mine = [to_owner(mine_grads, i) for i in range(2)]
    total_got = total_of(got_grads[0], owned_got)
    z2_in, owned_mine, total_got, dq_got, arriving = hold(
        z2_in, owned_mine, total_got, dq_got, arriving
    )

    z4 = total_of(z2, [z2_in])
    spans_back = [shift(z4, "y", r, NY) for r in ORDER]
    back = swap(jnp.concatenate([total_got, dq_got[None]]), "x")
    spans_back, back, mine_far = hold(spans_back, back, mine_grads[3])
    owned_mine.append(shift(mine_far, "y", -ORDER[2], NY))
    spans = jnp.stack([z4, *spans_back])
    spans_got, owned_mine = hold(swap(spans, "x"), owned_mine)
    ours = jnp.stack([spans, spans_got])
    model = out_weight.shape[1]
    half = model // 2
    weight_gradient = jnp.zeros((width, model), F32)
    for cr, block in enumerate((ours, swap(ours, "c"))):
        column = (c + cr) % 2 * half
        for i, r in enumerate((0, *ORDER)):
            for xr in range(2):
                row = (x + xr) % 2 * group + lax.rem(y - r + NY, NY) * span
                weight_gradient = lax.dynamic_update_slice(
                    weight_gradient, block[xr, i].astype(F32), (row, column)
                )

    layer_out = (residual[0].astype(F32) + kept + arriving.astype(F32)).astype(BF)
    total_mine = total_of(mine_grads[0], owned_mine)
    dq_mine = (dq_mine + dq_other[:rows]).astype(BF)
    kept_grads = jnp.concatenate([total_mine, dq_mine[None]])
    grad_keys, grad_values, grad_queries = by_x(x, kept_grads, back, 2)
    return (
        layer_out[None],
        grad_queries[None],
        grad_keys[None],
        grad_values[None],
        weight_gradient,
    )


def solution(mesh):
    fine = Mesh(mesh.devices.reshape(NZ, NY, 2, 2, 2), ("dp", "y", "x", "c", "tile"))
    rows = P("dp", ("y", "x", "c"), "tile")
    return jax.shard_map(
        body,
        mesh=fine,
        in_specs=(rows, rows, rows, rows, P("tile", None), rows),
        out_specs=(rows, rows, rows, rows, P("tile", None)),
        check_vma=False,
    )
```

```python
import jax
import jax.numpy as jnp
from jax import lax
from jax.experimental import pallas as pl
from jax.experimental.pallas import tpu as pltpu
from jax.sharding import Mesh
from jax.sharding import PartitionSpec as P

HD = 128
NY = 4
NZ = 8
ORDER = (1, 3, 2)
SCALE = HD**-0.5
LOG2E = 1.4426950408889634
FACTOR = SCALE * LOG2E
BF = jnp.bfloat16
F32 = jnp.float32
COST = pl.CostEstimate(flops=1, bytes_accessed=1, transcendentals=0)
PARAMS = pltpu.CompilerParams(vmem_limit_bytes=56 * 1024 * 1024)
IN_VMEM = pl.BlockSpec(memory_space=pltpu.VMEM)
IN_SMEM = pl.BlockSpec(memory_space=pltpu.SMEM)
RUN = 4
STATS = 8


def shift(value, axis, step, size):
    return lax.ppermute(value, axis, [(i, (i + step) % size) for i in range(size)])


def swap(value, axis):
    return shift(value, axis, 1, 2)


def hold(*values):
    return lax.optimization_barrier(values)


def dot(a, b, ca, cb):
    return lax.dot_general(a, b, (((ca,), (cb,)), ((), ())), preferred_element_type=F32)


def shaped(*shape, dtype=BF):
    return jax.ShapeDtypeStruct(shape, dtype)


def call(kernel, scalars, arrays, out_shape, scratch_shapes=()):
    return pl.pallas_call(
        kernel,
        in_specs=[IN_SMEM] * len(scalars) + [IN_VMEM] * len(arrays),
        out_specs=[IN_VMEM] * len(out_shape),
        out_shape=out_shape,
        scratch_shapes=list(scratch_shapes),
        compiler_params=PARAMS,
        cost_estimate=COST,
    )(*[s.reshape(1).astype(jnp.int32) for s in scalars], *arrays)


def split_kernel(x_ref, q, k, v, q_mine, q_theirs, kv_mine, kv_theirs):
    group = q_mine.shape[1]
    mine = pl.ds(pl.multiple_of(x_ref[0] * group, HD), group)
    theirs = pl.ds(pl.multiple_of((1 - x_ref[0]) * group, HD), group)
    kv_theirs[0] = k[:, theirs]
    kv_theirs[1] = v[:, theirs]
    kv_mine[0] = k[:, mine]
    kv_mine[1] = v[:, mine]
    q_mine[...] = q[:, mine]
    q_theirs[...] = q[:, theirs]


def split_heads(x, q, k, v):
    rows, width = q.shape
    one = shaped(rows, width // 2)
    two = shaped(2, rows, width // 2)
    return call(split_kernel, [x], [q, k, v], [one, one, two, two])


def head_columns(h):
    return slice(h * HD, (h + 1) * HD)


def stacked(refs, h):
    return jnp.concatenate([ref[:, head_columns(h)] for ref in refs], axis=0)


def arrays_of(blocks):
    return [array for block in blocks for array in block]


def blocks_of(refs, blocks):
    found, at = [], 0
    for block in blocks:
        found.append(refs[at : at + len(block)])
        at += len(block)
    return found


def run_of(blocks, which, h):
    columns = head_columns(h)
    return jnp.concatenate(
        [b[which][:, columns] if len(b) == 2 else b[0][which, :, columns] for b in blocks], axis=0
    )


def runs(kv):
    return [kv[i : i + RUN] for i in range(0, len(kv), RUN)]


def forward_kernel(blocks, heads, q0, q1, q2, q3, *refs):
    kv = runs(blocks_of(refs, blocks))
    own, other, scores_buf = refs[-3:]
    columns = 2 * q0.shape[0]
    tops = [jnp.full((1, 2 * columns), -jnp.inf, F32)] * heads

    def score(h, i):
        scores = dot(run_of(kv[i], 0, h), stacked((q0, q1, q2, q3), h), 1, 1) * FACTOR
        scores_buf[h % 2, i] = scores
        tops[h] = jnp.maximum(tops[h], jnp.max(scores, axis=0, keepdims=True))

    for i in range(len(kv)):
        score(0, i)
    for h in range(heads):
        total = jnp.zeros((1, 2 * columns), F32)
        acc = jnp.zeros((HD, 2 * columns), F32)
        for i in range(len(kv)):
            if h + 1 < heads:
                score(h + 1, i)
            weight = jnp.exp2(scores_buf[h % 2, i] - tops[h])
            total = total + jnp.sum(weight, axis=0, keepdims=True)
            acc = acc + dot(run_of(kv[i], 1, h), weight.astype(BF), 0, 0)
        pad = jnp.zeros((STATS - 2, 2 * columns), F32)
        stats = jnp.concatenate([tops[h], total, pad], axis=0)
        for out, part in ((own, slice(0, columns)), (other, slice(columns, 2 * columns))):
            out[h, :HD] = acc[:, part]
            out[h, HD:] = stats[:, part]


def merge_kernel(heads, own_ref, mine, got, g0, g1, cot0, cot1, tile0, tile1, *outs):
    out0, out1, stats, keep, send = outs
    rows = g0.shape[0]
    own = jnp.concatenate([cot0[...], cot1[...]], axis=0)
    tiles = jnp.concatenate([tile0[...], tile1[...]], axis=0)
    cot_keep = jnp.where(own_ref[0] == 1, own, tiles)
    cot_send = jnp.where(own_ref[0] == 1, tiles, own)
    for h in range(heads):
        top_a, total_a = mine[h, HD : HD + 1], mine[h, HD + 1 : HD + 2]
        top_b, total_b = got[h, HD : HD + 1], got[h, HD + 1 : HD + 2]
        top = jnp.maximum(top_a, top_b)
        scale_a, scale_b = jnp.exp2(top_a - top), jnp.exp2(top_b - top)
        total = total_a * scale_a + total_b * scale_b
        attended = (mine[h, :HD] * scale_a + got[h, :HD] * scale_b) / total
        delta = jnp.sum(
            attended * stacked((g0, g1), h).astype(F32).T, axis=0, keepdims=True
        )
        level = top + jnp.log2(total)
        pad = jnp.zeros((STATS - 2, 2 * rows), F32)
        stats[h] = jnp.concatenate([level, delta, pad], axis=0)
        rounded = attended.astype(BF)
        send[head_columns(h)] = dot(rounded, cot_send, 1, 0).astype(BF)
        keep[head_columns(h)] = dot(rounded, cot_keep, 1, 0).astype(BF)
        by_row = attended.T.astype(BF)
        out0[:, head_columns(h)] = by_row[:rows]
        out1[:, head_columns(h)] = by_row[rows:]


def forward(queries, kv):
    rows, width = queries[0].shape
    heads = width // HD
    return call(
        lambda *refs: forward_kernel(kv, heads, *refs),
        [],
        [*queries, *arrays_of(kv)],
        [shaped(heads, HD + STATS, 2 * rows, dtype=F32)] * 2,
        [pltpu.VMEM((2, len(runs(kv)), RUN * rows, 4 * rows), F32)],
    )


def merge(own, mine, got, grads, cots):
    rows, width = grads[0].shape
    heads = width // HD
    half = cots[0].shape[1]
    return call(
        lambda *refs: merge_kernel(heads, *refs),
        [own],
        [mine, got, *grads, *cots],
        [
            shaped(rows, width),
            shaped(rows, width),
            shaped(heads, STATS, 2 * rows, dtype=F32),
            shaped(width, half),
            shaped(width, half),
        ],
    )


def backward_kernel(blocks, heads, first, *refs):
    queries, grads, (stats_a, stats_b) = refs[:4], refs[4:8], refs[8:10]
    kv = blocks_of(refs[10:], blocks)
    at = 10 + len(arrays_of(blocks))
    outs = refs[at + (not first) :]
    rows = queries[0].shape[0]
    for h in range(heads):
        columns = head_columns(h)
        query = stacked(queries, h)
        grad = stacked(grads, h)
        stats = jnp.concatenate([stats_a[h], stats_b[h]], axis=1)
        level, delta = stats[0:1], stats[1:2]
        keys = run_of(kv, 0, h)
        prob = jnp.exp2(dot(keys, query, 1, 1) * FACTOR - level)
        dv = dot(prob.astype(BF), grad, 1, 0).astype(BF)
        dscore = (prob * (dot(run_of(kv, 1, h), grad, 1, 1) - delta)).astype(BF)
        dk = (dot(dscore, query, 1, 0) * SCALE).astype(BF)
        dq = dot(keys, dscore, 0, 0)
        for j in range(RUN):
            block = slice(j * rows, (j + 1) * rows)
            outs[j][0, :, columns] = dk[block]
            outs[j][1, :, columns] = dv[block]
        if first:
            outs[RUN][h] = dq
        else:
            dq_rows = ((dq + refs[at][h]) * SCALE).T
            outs[RUN][:, columns] = dq_rows[:rows]
            outs[RUN + 1][:, columns] = dq_rows[rows : 2 * rows]
            outs[RUN + 2][:, columns] = dq_rows[2 * rows :].astype(BF)


def backward(queries, grads, stats, kv, dq):
    rows, width = queries[0].shape
    heads = width // HD
    first = dq is None
    if first:
        dq_shapes = [shaped(heads, HD, 4 * rows, dtype=F32)]
    else:
        dq_shapes = [shaped(rows, width, dtype=F32)] * 2 + [shaped(2 * rows, width)]
    return call(
        lambda *refs: backward_kernel(kv, heads, first, *refs),
        [],
        [*queries, *grads, *stats, *arrays_of(kv)] + ([] if first else [dq]),
        [shaped(2, rows, width)] * RUN + dq_shapes,
    )


def by_x(x, mine, theirs, axis):
    return jnp.where(
        x == 0,
        jnp.concatenate([mine, theirs], axis=axis),
        jnp.concatenate([theirs, mine], axis=axis),
    )


def total_of(first, others):
    total = first.astype(F32)
    for value in others:
        total = total + value.astype(F32)
    return total.astype(BF)


def body(queries, key_vectors, value_vectors, residual, out_weight, cotangent):
    x = lax.axis_index("x")
    y = lax.axis_index("y")
    c = lax.axis_index("c")
    t = lax.axis_index("tile")
    width = queries.shape[2]
    group = width // 2

    query_mine, query_theirs, kv_mine, kv_theirs = split_heads(
        x, queries[0], key_vectors[0], value_vectors[0]
    )
    cot_own = cotangent[0]
    cot_own = cotangent[0]
    kv_got = swap(kv_theirs, "x")

    def gather_y(value):
        near = [shift(value, "y", r, NY) for r in ORDER[:2]]
        far = [shift(near[i][i], "y", ORDER[i], NY) for i in range(2)]
        return near, far

    mine_in, mine_far = gather_y(kv_mine)
    cot_other = swap(cot_own, "tile")
    query_mine_c = swap(query_mine, "c")
    got_in, got_far = gather_y(kv_got)
    mine_in, query_theirs, cot_sent = hold(mine_in, query_theirs, cot_own)
    query_got = swap(query_theirs, "x")
    query_got_c = swap(query_got, "c")
    cot_own_got = swap(cot_sent, "x")

    cot_other, mine_far, got_in = hold(cot_other, mine_far, got_in)

    def weight_columns(which):
        return lax.dynamic_slice_in_dim(out_weight, which * width, width, 1)

    attention_gradient = (
        dot(cot_own, weight_columns(t), 1, 1) + dot(cot_other, weight_columns(1 - t), 1, 1)
    ).astype(BF)
    grad_mine = lax.dynamic_slice_in_dim(attention_gradient, x * group, group, 1)
    grad_theirs = lax.dynamic_slice_in_dim(attention_gradient, (1 - x) * group, group, 1)
    grad_got = swap(grad_theirs, "x")
    cot_other_got = swap(cot_other, "x")
    mine_in, got_in, mine_far, got_far, query_mine_c, query_got_c, grad_theirs = hold(
        mine_in, got_in, mine_far, got_far, query_mine_c, query_got_c, grad_theirs
    )
    queries_all = [query_mine, query_got, query_mine_c, query_got_c]
    mine_blocks = [[kv_mine], [mine_in[0]], [mine_in[1]], mine_far]
    got_blocks = [[kv_got], [got_in[0]], [got_in[1]], got_far]
    mine, others = forward(queries_all, mine_blocks + got_blocks)
    grad_mine_c = swap(grad_mine, "c")
    mine, others, grad_got, cot_own_got, cot_other_got, grad_mine_c = hold(
        mine, others, grad_got, cot_own_got, cot_other_got, grad_mine_c
    )
    merged = swap(others, "c")
    grad_got_c = swap(grad_got, "c")
    merged, grad_got_c = hold(merged, grad_got_c)
    out_mine, out_got, stats, keep, send = hold(
        *merge(
            c == t,
            mine,
            merged,
            [grad_mine, grad_got],
            [cot_own, cot_own_got, cot_other, cot_other_got],
        )
    )

    stats_c = swap(stats, "c")
    part = total_of(keep, [swap(send, "c")])
    span = group // NY
    spans_out = [
        lax.dynamic_slice_in_dim(part, lax.rem(y + r, NY) * span, span, 0) for r in (0, *ORDER)
    ]

    def to_owner(blocks, i):
        return shift(blocks[i + 1], "y", -ORDER[i], NY)

    def from_z(value, bit):
        return lax.ppermute(value, "dp", [(i, i ^ bit) for i in range(NZ)])

    spans_out, stats_c, out_got, query_mine = hold(spans_out, stats_c, out_got, query_mine)
    spans_in = [shift(v, "y", r, NY) for v, r in zip(spans_out[1:], ORDER)]
    out_back = swap(out_got, "x")
    grads_all = [grad_mine, grad_got, grad_mine_c, grad_got_c]
    rest = (grads_all, [stats, stats_c])
    got_grads = backward([query_mine, *queries_all[1:]], *rest, got_blocks, None)
    got_grads, spans_in, out_back = hold(got_grads, spans_in, out_back)

    z0, query_mine = hold(total_of(spans_out[0], spans_in), query_mine)
    z0_in = from_z(z0, 1)
    owned_got = [to_owner(got_grads, i) for i in range(2)]
    mine_grads = backward(
        [query_mine, *queries_all[1:]], *rest, mine_blocks, got_grads[RUN]
    )
    mine_grads, z0_in, out_mine = hold(mine_grads, z0_in, out_mine)
    dq_mine, dq_got, dq_other = mine_grads[RUN:]

    z1, out_mine, dq_other = hold(total_of(z0, [z0_in]), out_mine, dq_other)
    z1_in = from_z(z1, 2)
    owned_got.append(to_owner(got_grads, 2))
    dq_other = swap(dq_other, "c").astype(F32)
    rows = dq_mine.shape[0]
    attended = by_x(x, out_mine, out_back, 1)
    projected = dot(attended, out_weight, 1, 0)
    kept = lax.dynamic_slice_in_dim(projected, t * width, width, 1)
    leaving = lax.dynamic_slice_in_dim(projected, (1 - t) * width, width, 1).astype(BF)
    dq_got = (dq_got + dq_other[rows:]).astype(BF)
    z1_in, leaving, owned_got[0], owned_got[1], dq_got = hold(
        z1_in, leaving, owned_got[0], owned_got[1], dq_got
    )

    z2 = total_of(z1, [z1_in])
    z2_in = from_z(z2, 4)
    arriving = swap(leaving, "tile")
    owned_mine = [to_owner(mine_grads, i) for i in range(2)]
    total_got = total_of(got_grads[0], owned_got)
    dq_back = swap(dq_got, "x")
    z2_in, total_got, dq_back, arriving = hold(z2_in, total_got, dq_back, arriving)

    z4 = total_of(z2, [z2_in])
    spans_back = [shift(z4, "y", r, NY) for r in ORDER]
    z4_got = swap(z4, "x")
    back = swap(total_got, "x")
    spans_back, back, z4_got, leaving_far = hold(spans_back, back, z4_got, mine_grads[3])
    owned_mine.append(shift(leaving_far, "y", -ORDER[2], NY))
    spans_got, owned_mine = hold(swap(jnp.stack(spans_back), "x"), owned_mine)
    ours = jnp.stack([z4, *spans_back, z4_got, *[spans_got[i] for i in range(NY - 1)]])
    model = out_weight.shape[1]
    half = model // 2
    weight_gradient = jnp.zeros((width, model), F32)
    for cr, block in enumerate((ours, swap(ours, "c"))):
        column = (c + cr) % 2 * half
        for i, r in enumerate((0, *ORDER)):
            for xr in range(2):
                row = (x + xr) % 2 * group + lax.rem(y - r + NY, NY) * span
                weight_gradient = lax.dynamic_update_slice(
                    weight_gradient, block[xr * NY + i].astype(F32), (row, column)
                )

    layer_out = (residual[0].astype(F32) + kept + arriving.astype(F32)).astype(BF)
    total_mine = total_of(mine_grads[0], owned_mine)
    dq_mine = (dq_mine + dq_other[:rows]).astype(BF)
    grad_queries = by_x(x, dq_mine, dq_back, 1)
    grad_keys, grad_values = by_x(x, total_mine, back, 2)
    return (
        layer_out[None],
        grad_queries[None],
        grad_keys[None],
        grad_values[None],
        weight_gradient,
    )


def solution(mesh):
    fine = Mesh(mesh.devices.reshape(NZ, NY, 2, 2, 2), ("dp", "y", "x", "c", "tile"))
    rows = P("dp", ("y", "x", "c"), "tile")
    return jax.shard_map(
        body,
        mesh=fine,
        in_specs=(rows, rows, rows, rows, P("tile", None), rows),
        out_specs=(rows, rows, rows, rows, P("tile", None)),
        check_vma=False,
    )
```

```python
import jax
import jax.numpy as jnp
from jax import lax
from jax.experimental import pallas as pl
from jax.experimental.pallas import tpu as pltpu
from jax.sharding import Mesh
from jax.sharding import PartitionSpec as P

HD = 128
NY = 4
NZ = 8
ORDER = (1, 3, 2)
SCALE = HD**-0.5
LOG2E = 1.4426950408889634
FACTOR = SCALE * LOG2E
BF = jnp.bfloat16
F32 = jnp.float32
COST = pl.CostEstimate(flops=1, bytes_accessed=1, transcendentals=0)
PARAMS = pltpu.CompilerParams(vmem_limit_bytes=56 * 1024 * 1024)
IN_VMEM = pl.BlockSpec(memory_space=pltpu.VMEM)
IN_SMEM = pl.BlockSpec(memory_space=pltpu.SMEM)
RUN = 4
STATS = 8


def shift(value, axis, step, size):
    return lax.ppermute(value, axis, [(i, (i + step) % size) for i in range(size)])


def swap(value, axis):
    return shift(value, axis, 1, 2)


def hold(*values):
    return lax.optimization_barrier(values)


def dot(a, b, ca, cb):
    return lax.dot_general(a, b, (((ca,), (cb,)), ((), ())), preferred_element_type=F32)


def shaped(*shape, dtype=BF):
    return jax.ShapeDtypeStruct(shape, dtype)


def call(kernel, scalars, arrays, out_shape, scratch_shapes=()):
    return pl.pallas_call(
        kernel,
        in_specs=[IN_SMEM] * len(scalars) + [IN_VMEM] * len(arrays),
        out_specs=[IN_VMEM] * len(out_shape),
        out_shape=out_shape,
        scratch_shapes=list(scratch_shapes),
        compiler_params=PARAMS,
        cost_estimate=COST,
    )(*[s.reshape(1).astype(jnp.int32) for s in scalars], *arrays)


def split_kernel(x_ref, q, k, v, q_mine, q_theirs, kv_mine, kv_theirs):
    group = q_mine.shape[1]
    mine = pl.ds(pl.multiple_of(x_ref[0] * group, HD), group)
    theirs = pl.ds(pl.multiple_of((1 - x_ref[0]) * group, HD), group)
    kv_theirs[0] = k[:, theirs]
    kv_theirs[1] = v[:, theirs]
    kv_mine[0] = k[:, mine]
    kv_mine[1] = v[:, mine]
    q_mine[...] = q[:, mine]
    q_theirs[...] = q[:, theirs]


def split_heads(x, q, k, v):
    rows, width = q.shape
    one = shaped(rows, width // 2)
    two = shaped(2, rows, width // 2)
    return call(split_kernel, [x], [q, k, v], [one, one, two, two])


def head_columns(h):
    return slice(h * HD, (h + 1) * HD)


def stacked(refs, h):
    return jnp.concatenate([ref[:, head_columns(h)] for ref in refs], axis=0)


def run_of(refs, which, h):
    return jnp.concatenate([ref[which, :, head_columns(h)] for ref in refs], axis=0)


def runs(kv):
    return [kv[i : i + RUN] for i in range(0, len(kv), RUN)]


def forward_kernel(n_kv, heads, q0, q1, q2, q3, *refs):
    kv = runs(refs[:n_kv])
    own, other, scores_buf = refs[n_kv:]
    columns = 2 * q0.shape[0]
    tops = [jnp.full((1, 2 * columns), -jnp.inf, F32)] * heads

    def score(h, i):
        scores = dot(run_of(kv[i], 0, h), stacked((q0, q1, q2, q3), h), 1, 1) * FACTOR
        scores_buf[h % 2, i] = scores
        tops[h] = jnp.maximum(tops[h], jnp.max(scores, axis=0, keepdims=True))

    for i in range(len(kv)):
        score(0, i)
    for h in range(heads):
        total = jnp.zeros((1, 2 * columns), F32)
        acc = jnp.zeros((HD, 2 * columns), F32)
        for i in range(len(kv)):
            if h + 1 < heads:
                score(h + 1, i)
            weight = jnp.exp2(scores_buf[h % 2, i] - tops[h])
            total = total + jnp.sum(weight, axis=0, keepdims=True)
            acc = acc + dot(run_of(kv[i], 1, h), weight.astype(BF), 0, 0)
        pad = jnp.zeros((STATS - 2, 2 * columns), F32)
        stats = jnp.concatenate([tops[h], total, pad], axis=0)
        for out, part in ((own, slice(0, columns)), (other, slice(columns, 2 * columns))):
            out[h, :HD] = acc[:, part]
            out[h, HD:] = stats[:, part]


def merge_kernel(heads, own_ref, mine, got, g0, g1, cot0, cot1, tile0, tile1, *outs):
    out0, out1, stats, keep, send = outs
    rows = g0.shape[0]
    own = jnp.concatenate([cot0[...], cot1[...]], axis=0)
    tiles = jnp.concatenate([tile0[...], tile1[...]], axis=0)
    cot_keep = jnp.where(own_ref[0] == 1, own, tiles)
    cot_send = jnp.where(own_ref[0] == 1, tiles, own)
    for h in range(heads):
        top_a, total_a = mine[h, HD : HD + 1], mine[h, HD + 1 : HD + 2]
        top_b, total_b = got[h, HD : HD + 1], got[h, HD + 1 : HD + 2]
        top = jnp.maximum(top_a, top_b)
        scale_a, scale_b = jnp.exp2(top_a - top), jnp.exp2(top_b - top)
        total = total_a * scale_a + total_b * scale_b
        attended = (mine[h, :HD] * scale_a + got[h, :HD] * scale_b) / total
        delta = jnp.sum(
            attended * stacked((g0, g1), h).astype(F32).T, axis=0, keepdims=True
        )
        level = top + jnp.log2(total)
        pad = jnp.zeros((STATS - 2, 2 * rows), F32)
        stats[h] = jnp.concatenate([level, delta, pad], axis=0)
        rounded = attended.astype(BF)
        send[head_columns(h)] = dot(rounded, cot_send, 1, 0).astype(BF)
        keep[head_columns(h)] = dot(rounded, cot_keep, 1, 0).astype(BF)
        by_row = attended.T.astype(BF)
        out0[:, head_columns(h)] = by_row[:rows]
        out1[:, head_columns(h)] = by_row[rows:]


def forward(queries, kv):
    rows, width = queries[0].shape
    heads = width // HD
    return call(
        lambda *refs: forward_kernel(len(kv), heads, *refs),
        [],
        [*queries, *kv],
        [shaped(heads, HD + STATS, 2 * rows, dtype=F32)] * 2,
        [pltpu.VMEM((2, len(runs(kv)), RUN * rows, 4 * rows), F32)],
    )


def merge(own, mine, got, grads, cots):
    rows, width = grads[0].shape
    heads = width // HD
    half = cots[0].shape[1]
    return call(
        lambda *refs: merge_kernel(heads, *refs),
        [own],
        [mine, got, *grads, *cots],
        [
            shaped(rows, width),
            shaped(rows, width),
            shaped(heads, STATS, 2 * rows, dtype=F32),
            shaped(width, half),
            shaped(width, half),
        ],
    )


def backward_kernel(heads, first, *refs):
    queries, grads, (stats_a, stats_b), kv = refs[:4], refs[4:8], refs[8:10], refs[10 : 10 + RUN]
    outs = refs[10 + RUN + (not first) :]
    rows = queries[0].shape[0]
    for h in range(heads):
        columns = head_columns(h)
        query = stacked(queries, h)
        grad = stacked(grads, h)
        stats = jnp.concatenate([stats_a[h], stats_b[h]], axis=1)
        level, delta = stats[0:1], stats[1:2]
        keys = run_of(kv, 0, h)
        prob = jnp.exp2(dot(keys, query, 1, 1) * FACTOR - level)
        dv = dot(prob.astype(BF), grad, 1, 0).astype(BF)
        dscore = (prob * (dot(run_of(kv, 1, h), grad, 1, 1) - delta)).astype(BF)
        dk = (dot(dscore, query, 1, 0) * SCALE).astype(BF)
        dq = dot(keys, dscore, 0, 0)
        for j in range(RUN):
            block = slice(j * rows, (j + 1) * rows)
            outs[j][0, :, columns] = dk[block]
            outs[j][1, :, columns] = dv[block]
        if first:
            outs[RUN][h] = dq
        else:
            dq_rows = ((dq + refs[10 + RUN][h]) * SCALE).T
            outs[RUN][:, columns] = dq_rows[:rows]
            outs[RUN + 1][:, columns] = dq_rows[rows : 2 * rows]
            outs[RUN + 2][:, columns] = dq_rows[2 * rows :].astype(BF)


def backward(queries, grads, stats, kv, dq):
    rows, width = queries[0].shape
    heads = width // HD
    first = dq is None
    if first:
        dq_shapes = [shaped(heads, HD, 4 * rows, dtype=F32)]
    else:
        dq_shapes = [shaped(rows, width, dtype=F32)] * 2 + [shaped(2 * rows, width)]
    return call(
        lambda *refs: backward_kernel(heads, first, *refs),
        [],
        [*queries, *grads, *stats, *kv] + ([] if first else [dq]),
        [shaped(2, rows, width)] * RUN + dq_shapes,
    )


def by_x(x, mine, theirs, axis):
    return jnp.where(
        x == 0,
        jnp.concatenate([mine, theirs], axis=axis),
        jnp.concatenate([theirs, mine], axis=axis),
    )


def total_of(first, others):
    total = first.astype(F32)
    for value in others:
        total = total + value.astype(F32)
    return total.astype(BF)


def body(queries, key_vectors, value_vectors, residual, out_weight, cotangent):
    x = lax.axis_index("x")
    y = lax.axis_index("y")
    c = lax.axis_index("c")
    t = lax.axis_index("tile")
    width = queries.shape[2]
    group = width // 2

    query_mine, query_theirs, kv_mine, kv_theirs = split_heads(
        x, queries[0], key_vectors[0], value_vectors[0]
    )
    cot_own = cotangent[0]
    cot_own = cotangent[0]
    kv_got = swap(kv_theirs, "x")
    mine_in = [shift(kv_mine, "y", r, NY) for r in ORDER]
    cot_other = swap(cot_own, "tile")
    query_mine_c = swap(query_mine, "c")
    kv_got, query_theirs, cot_sent = hold(kv_got, query_theirs, cot_own)
    got_in = [shift(kv_got, "y", r, NY) for r in ORDER]
    query_got = swap(query_theirs, "x")
    query_got_c = swap(query_got, "c")
    cot_own_got = swap(cot_sent, "x")

    def weight_columns(which):
        return lax.dynamic_slice_in_dim(out_weight, which * width, width, 1)

    attention_gradient = (
        dot(cot_own, weight_columns(t), 1, 1) + dot(cot_other, weight_columns(1 - t), 1, 1)
    ).astype(BF)
    grad_mine = lax.dynamic_slice_in_dim(attention_gradient, x * group, group, 1)
    grad_theirs = lax.dynamic_slice_in_dim(attention_gradient, (1 - x) * group, group, 1)
    grad_got = swap(grad_theirs, "x")
    cot_other_got = swap(cot_other, "x")
    mine_in, got_in, query_mine_c, query_got_c, grad_theirs = hold(
        mine_in, got_in, query_mine_c, query_got_c, grad_theirs
    )
    queries_all = [query_mine, query_got, query_mine_c, query_got_c]
    mine, others = forward(queries_all, [kv_mine, *mine_in, kv_got, *got_in])
    grad_mine_c = swap(grad_mine, "c")
    mine, others, grad_got, cot_own_got, cot_other_got, grad_mine_c = hold(
        mine, others, grad_got, cot_own_got, cot_other_got, grad_mine_c
    )
    merged = swap(others, "c")
    grad_got_c = swap(grad_got, "c")
    merged, grad_got_c = hold(merged, grad_got_c)
    out_mine, out_got, stats, keep, send = hold(
        *merge(
            c == t,
            mine,
            merged,
            [grad_mine, grad_got],
            [cot_own, cot_own_got, cot_other, cot_other_got],
        )
    )

    stats_c = swap(stats, "c")
    part = total_of(keep, [swap(send, "c")])
    span = group // NY
    spans_out = [
        lax.dynamic_slice_in_dim(part, lax.rem(y + r, NY) * span, span, 0) for r in (0, *ORDER)
    ]

    def to_owner(blocks, i):
        return shift(blocks[i + 1], "y", -ORDER[i], NY)

    def from_z(value, bit):
        return lax.ppermute(value, "dp", [(i, i ^ bit) for i in range(NZ)])

    spans_out, stats_c, out_got, query_mine = hold(spans_out, stats_c, out_got, query_mine)
    spans_in = [shift(v, "y", r, NY) for v, r in zip(spans_out[1:], ORDER)]
    out_back = swap(out_got, "x")
    grads_all = [grad_mine, grad_got, grad_mine_c, grad_got_c]
    rest = (grads_all, [stats, stats_c])
    got_grads = backward([query_mine, *queries_all[1:]], *rest, [kv_got, *got_in], None)
    got_grads, spans_in, out_back = hold(got_grads, spans_in, out_back)

    z0, query_mine = hold(total_of(spans_out[0], spans_in), query_mine)
    z0_in = from_z(z0, 1)
    owned_got = [to_owner(got_grads, i) for i in range(2)]
    mine_grads = backward(
        [query_mine, *queries_all[1:]], *rest, [kv_mine, *mine_in], got_grads[RUN]
    )
    mine_grads, z0_in, out_mine = hold(mine_grads, z0_in, out_mine)
    dq_mine, dq_got, dq_other = mine_grads[RUN:]

    z1, out_mine, dq_other = hold(total_of(z0, [z0_in]), out_mine, dq_other)
    z1_in = from_z(z1, 2)
    owned_got.append(to_owner(got_grads, 2))
    dq_other = swap(dq_other, "c").astype(F32)
    rows = dq_mine.shape[0]
    attended = by_x(x, out_mine, out_back, 1)
    projected = dot(attended, out_weight, 1, 0)
    kept = lax.dynamic_slice_in_dim(projected, t * width, width, 1)
    leaving = lax.dynamic_slice_in_dim(projected, (1 - t) * width, width, 1).astype(BF)
    dq_got = (dq_got + dq_other[rows:]).astype(BF)
    z1_in, leaving, owned_got[0], owned_got[1], dq_got = hold(
        z1_in, leaving, owned_got[0], owned_got[1], dq_got
    )

    z2 = total_of(z1, [z1_in])
    z2_in = from_z(z2, 4)
    arriving = swap(leaving, "tile")
    owned_mine = [to_owner(mine_grads, i) for i in range(2)]
    total_got = total_of(got_grads[0], owned_got)
    z2_in, owned_mine, total_got, dq_got, arriving = hold(
        z2_in, owned_mine, total_got, dq_got, arriving
    )

    z4 = total_of(z2, [z2_in])
    spans_back = [shift(z4, "y", r, NY) for r in ORDER]
    back = swap(jnp.concatenate([total_got, dq_got[None]]), "x")
    spans_back, back, mine_far = hold(spans_back, back, mine_grads[3])
    owned_mine.append(shift(mine_far, "y", -ORDER[2], NY))
    spans = jnp.stack([z4, *spans_back])
    spans_got, owned_mine = hold(swap(spans, "x"), owned_mine)
    ours = jnp.stack([spans, spans_got])
    model = out_weight.shape[1]
    half = model // 2
    weight_gradient = jnp.zeros((width, model), F32)
    for cr, block in enumerate((ours, swap(ours, "c"))):
        column = (c + cr) % 2 * half
        for i, r in enumerate((0, *ORDER)):
            for xr in range(2):
                row = (x + xr) % 2 * group + lax.rem(y - r + NY, NY) * span
                weight_gradient = lax.dynamic_update_slice(
                    weight_gradient, block[xr, i].astype(F32), (row, column)
                )

    layer_out = (residual[0].astype(F32) + kept + arriving.astype(F32)).astype(BF)
    total_mine = total_of(mine_grads[0], owned_mine)
    dq_mine = (dq_mine + dq_other[:rows]).astype(BF)
    kept_grads = jnp.concatenate([total_mine, dq_mine[None]])
    grad_keys, grad_values, grad_queries = by_x(x, kept_grads, back, 2)
    return (
        layer_out[None],
        grad_queries[None],
        grad_keys[None],
        grad_values[None],
        weight_gradient,
    )


def solution(mesh):
    fine = Mesh(mesh.devices.reshape(NZ, NY, 2, 2, 2), ("dp", "y", "x", "c", "tile"))
    rows = P("dp", ("y", "x", "c"), "tile")
    return jax.shard_map(
        body,
        mesh=fine,
        in_specs=(rows, rows, rows, rows, P("tile", None), rows),
        out_specs=(rows, rows, rows, rows, P("tile", None)),
        check_vma=False,
    )
```

```python
import jax
import jax.numpy as jnp
from jax import lax
from jax.experimental import pallas as pl
from jax.experimental.pallas import tpu as pltpu
from jax.sharding import Mesh
from jax.sharding import PartitionSpec as P

HD = 128
NY = 4
NZ = 8
ORDER = (1, 3, 2)
SCALE = HD**-0.5
LOG2E = 1.4426950408889634
FACTOR = SCALE * LOG2E
BF = jnp.bfloat16
F32 = jnp.float32
COST = pl.CostEstimate(flops=1, bytes_accessed=1, transcendentals=0)
MIB = 1024 * 1024
IN_VMEM = pl.BlockSpec(memory_space=pltpu.VMEM)
IN_SMEM = pl.BlockSpec(memory_space=pltpu.SMEM)
RUN = 4
STATS = 8


def shift(value, axis, step, size):
    return lax.ppermute(value, axis, [(i, (i + step) % size) for i in range(size)])


def swap(value, axis):
    return shift(value, axis, 1, 2)


def hold(*values):
    return lax.optimization_barrier(values)


def dot(a, b, ca, cb):
    return lax.dot_general(a, b, (((ca,), (cb,)), ((), ())), preferred_element_type=F32)


def shaped(*shape, dtype=BF):
    return jax.ShapeDtypeStruct(shape, dtype)


def call(kernel, vmem, scalars, arrays, out_shape, scratch_shapes=()):
    return pl.pallas_call(
        kernel,
        in_specs=[IN_SMEM] * len(scalars) + [IN_VMEM] * len(arrays),
        out_specs=[IN_VMEM] * len(out_shape),
        out_shape=out_shape,
        scratch_shapes=list(scratch_shapes),
        compiler_params=pltpu.CompilerParams(vmem_limit_bytes=vmem),
        cost_estimate=COST,
    )(*[s.reshape(1).astype(jnp.int32) for s in scalars], *arrays)


def split_kernel(x_ref, q, k, v, q_mine, q_theirs, kv_mine, kv_theirs):
    group = q_mine.shape[1]
    mine = pl.ds(pl.multiple_of(x_ref[0] * group, HD), group)
    theirs = pl.ds(pl.multiple_of((1 - x_ref[0]) * group, HD), group)
    kv_theirs[0] = k[:, theirs]
    kv_theirs[1] = v[:, theirs]
    kv_mine[0] = k[:, mine]
    kv_mine[1] = v[:, mine]
    q_mine[...] = q[:, mine]
    q_theirs[...] = q[:, theirs]


def split_heads(x, q, k, v):
    rows, width = q.shape
    one = shaped(rows, width // 2)
    two = shaped(2, rows, width // 2)
    return call(split_kernel, 62 * MIB, [x], [q, k, v], [one, one, two, two])


def head_columns(h):
    return slice(h * HD, (h + 1) * HD)


def stacked(refs, h):
    return jnp.concatenate([ref[:, head_columns(h)] for ref in refs], axis=0)


def arrays_of(blocks):
    return [array for block in blocks for array in block]


def blocks_of(refs, blocks):
    found, at = [], 0
    for block in blocks:
        found.append(refs[at : at + len(block)])
        at += len(block)
    return found


def run_of(blocks, which, h):
    columns = head_columns(h)
    return jnp.concatenate(
        [b[which][:, columns] if len(b) == 2 else b[0][which, :, columns] for b in blocks], axis=0
    )


def runs(kv):
    return [kv[i : i + RUN] for i in range(0, len(kv), RUN)]


def forward_kernel(blocks, heads, q0, q1, q2, q3, *refs):
    kv = runs(blocks_of(refs, blocks))
    own, other, scores_buf = refs[-3:]
    columns = 2 * q0.shape[0]
    tops = [jnp.full((1, 2 * columns), -jnp.inf, F32)] * heads

    def score(h, i):
        scores = dot(run_of(kv[i], 0, h), stacked((q0, q1, q2, q3), h), 1, 1) * FACTOR
        scores_buf[h % 2, i] = scores
        tops[h] = jnp.maximum(tops[h], jnp.max(scores, axis=0, keepdims=True))

    for i in range(len(kv)):
        score(0, i)
    for h in range(heads):
        total = jnp.zeros((1, 2 * columns), F32)
        acc = jnp.zeros((HD, 2 * columns), F32)
        for i in range(len(kv)):
            if h + 1 < heads:
                score(h + 1, i)
            weight = jnp.exp2(scores_buf[h % 2, i] - tops[h])
            total = total + jnp.sum(weight, axis=0, keepdims=True)
            acc = acc + dot(run_of(kv[i], 1, h), weight.astype(BF), 0, 0)
        pad = jnp.zeros((STATS - 2, 2 * columns), F32)
        stats = jnp.concatenate([tops[h], total, pad], axis=0)
        for out, part in ((own, slice(0, columns)), (other, slice(columns, 2 * columns))):
            out[h, :HD] = acc[:, part]
            out[h, HD:] = stats[:, part]


def merge_kernel(heads, own_ref, mine, got, g0, g1, cot0, cot1, tile0, tile1, *outs):
    out0, out1, stats, keep, send = outs
    rows = g0.shape[0]
    own = jnp.concatenate([cot0[...], cot1[...]], axis=0)
    tiles = jnp.concatenate([tile0[...], tile1[...]], axis=0)
    cot_keep = jnp.where(own_ref[0] == 1, own, tiles)
    cot_send = jnp.where(own_ref[0] == 1, tiles, own)
    for h in range(heads):
        top_a, total_a = mine[h, HD : HD + 1], mine[h, HD + 1 : HD + 2]
        top_b, total_b = got[h, HD : HD + 1], got[h, HD + 1 : HD + 2]
        top = jnp.maximum(top_a, top_b)
        scale_a, scale_b = jnp.exp2(top_a - top), jnp.exp2(top_b - top)
        total = total_a * scale_a + total_b * scale_b
        attended = (mine[h, :HD] * scale_a + got[h, :HD] * scale_b) / total
        delta = jnp.sum(
            attended * stacked((g0, g1), h).astype(F32).T, axis=0, keepdims=True
        )
        level = top + jnp.log2(total)
        pad = jnp.zeros((STATS - 2, 2 * rows), F32)
        stats[h] = jnp.concatenate([level, delta, pad], axis=0)
        rounded = attended.astype(BF)
        send[head_columns(h)] = dot(rounded, cot_send, 1, 0).astype(BF)
        keep[head_columns(h)] = dot(rounded, cot_keep, 1, 0).astype(BF)
        by_row = attended.T.astype(BF)
        out0[:, head_columns(h)] = by_row[:rows]
        out1[:, head_columns(h)] = by_row[rows:]


def forward(queries, kv):
    rows, width = queries[0].shape
    heads = width // HD
    return call(
        lambda *refs: forward_kernel(kv, heads, *refs),
        62 * MIB,
        [],
        [*queries, *arrays_of(kv)],
        [shaped(heads, HD + STATS, 2 * rows, dtype=F32)] * 2,
        [pltpu.VMEM((2, len(runs(kv)), RUN * rows, 4 * rows), F32)],
    )


def merge(own, mine, got, grads, cots):
    rows, width = grads[0].shape
    heads = width // HD
    half = cots[0].shape[1]
    return call(
        lambda *refs: merge_kernel(heads, *refs),
        62 * MIB,
        [own],
        [mine, got, *grads, *cots],
        [
            shaped(rows, width),
            shaped(rows, width),
            shaped(heads, STATS, 2 * rows, dtype=F32),
            shaped(width, half),
            shaped(width, half),
        ],
    )


def backward_kernel(blocks, heads, first, *refs):
    queries, grads, (stats_a, stats_b) = refs[:4], refs[4:8], refs[8:10]
    kv = blocks_of(refs[10:], blocks)
    at = 10 + len(arrays_of(blocks))
    outs = refs[at + (not first) :]
    rows = queries[0].shape[0]
    for h in range(heads):
        columns = head_columns(h)
        query = stacked(queries, h)
        grad = stacked(grads, h)
        stats = jnp.concatenate([stats_a[h], stats_b[h]], axis=1)
        level, delta = stats[0:1], stats[1:2]
        keys = run_of(kv, 0, h)
        prob = jnp.exp2(dot(keys, query, 1, 1) * FACTOR - level)
        dv = dot(prob.astype(BF), grad, 1, 0).astype(BF)
        dscore = (prob * (dot(run_of(kv, 1, h), grad, 1, 1) - delta)).astype(BF)
        dk = (dot(dscore, query, 1, 0) * SCALE).astype(BF)
        dq = dot(keys, dscore, 0, 0)
        for j in range(RUN):
            block = slice(j * rows, (j + 1) * rows)
            outs[j][0, :, columns] = dk[block]
            outs[j][1, :, columns] = dv[block]
        if first:
            outs[RUN][h] = dq
        else:
            dq_rows = ((dq + refs[at][h]) * SCALE).T
            outs[RUN][:, columns] = dq_rows[:rows]
            outs[RUN + 1][:, columns] = dq_rows[rows : 2 * rows]
            outs[RUN + 2][:, columns] = dq_rows[2 * rows :].astype(BF)


def backward(queries, grads, stats, kv, dq):
    rows, width = queries[0].shape
    heads = width // HD
    first = dq is None
    if first:
        dq_shapes = [shaped(heads, HD, 4 * rows, dtype=F32)]
    else:
        dq_shapes = [shaped(rows, width, dtype=F32)] * 2 + [shaped(2 * rows, width)]
    return call(
        lambda *refs: backward_kernel(kv, heads, first, *refs),
        62 * MIB,
        [],
        [*queries, *grads, *stats, *arrays_of(kv)] + ([] if first else [dq]),
        [shaped(2, rows, width)] * RUN + dq_shapes,
    )


def by_x(x, mine, theirs, axis):
    return jnp.where(
        x == 0,
        jnp.concatenate([mine, theirs], axis=axis),
        jnp.concatenate([theirs, mine], axis=axis),
    )


def total_of(first, others):
    total = first.astype(F32)
    for value in others:
        total = total + value.astype(F32)
    return total.astype(BF)


def body(queries, key_vectors, value_vectors, residual, out_weight, cotangent):
    x = lax.axis_index("x")
    y = lax.axis_index("y")
    c = lax.axis_index("c")
    t = lax.axis_index("tile")
    width = queries.shape[2]
    group = width // 2

    query_mine, query_theirs, kv_mine, kv_theirs = split_heads(
        x, queries[0], key_vectors[0], value_vectors[0]
    )
    cot_own = cotangent[0]
    cot_own = cotangent[0]
    kv_got = swap(kv_theirs, "x")

    def near_y(value):
        return [shift(value, "y", r, NY) for r in ORDER[:2]]

    def far_y(near):
        return [shift(near[i][i], "y", ORDER[i], NY) for i in range(2)]

    mine_in = near_y(kv_mine)
    query_mine_c = swap(query_mine, "c")
    kv_got, query_theirs, cot_sent = hold(kv_got, query_theirs, cot_own)
    got_in = near_y(kv_got)
    mine_in, kv_got = hold(mine_in, kv_got)
    mine_far = far_y(mine_in)
    got_far = far_y(got_in)
    query_got = swap(query_theirs, "x")
    cot_other = swap(cot_sent, "tile")
    query_got, mine_far = hold(query_got, mine_far)
    query_got_c = swap(query_got, "c")
    cot_own_got = swap(cot_sent, "x")

    cot_other, mine_far, got_in = hold(cot_other, mine_far, got_in)

    def weight_columns(which):
        return lax.dynamic_slice_in_dim(out_weight, which * width, width, 1)

    attention_gradient = (
        dot(cot_own, weight_columns(t), 1, 1) + dot(cot_other, weight_columns(1 - t), 1, 1)
    ).astype(BF)
    grad_mine = lax.dynamic_slice_in_dim(attention_gradient, x * group, group, 1)
    grad_theirs = lax.dynamic_slice_in_dim(attention_gradient, (1 - x) * group, group, 1)
    grad_got = swap(grad_theirs, "x")
    cot_other_got = swap(cot_other, "x")
    mine_in, got_in, mine_far, got_far, query_mine_c, query_got_c, grad_theirs = hold(
        mine_in, got_in, mine_far, got_far, query_mine_c, query_got_c, grad_theirs
    )
    queries_all = [query_mine, query_got, query_mine_c, query_got_c]
    mine_blocks = [[kv_mine], [mine_in[0]], [mine_in[1]], mine_far]
    got_blocks = [[kv_got], [got_in[0]], [got_in[1]], got_far]
    mine, others = forward(queries_all, mine_blocks + got_blocks)
    grad_mine_c = swap(grad_mine, "c")
    mine, others, grad_got, cot_own_got, cot_other_got, grad_mine_c = hold(
        mine, others, grad_got, cot_own_got, cot_other_got, grad_mine_c
    )
    merged = swap(others, "c")
    grad_got_c = swap(grad_got, "c")
    merged, grad_got_c = hold(merged, grad_got_c)
    out_mine, out_got, stats, keep, send = hold(
        *merge(
            c == t,
            mine,
            merged,
            [grad_mine, grad_got],
            [cot_own, cot_own_got, cot_other, cot_other_got],
        )
    )

    stats_c = swap(stats, "c")
    part = total_of(keep, [swap(send, "c")])
    span = group // NY
    spans_out = [
        lax.dynamic_slice_in_dim(part, lax.rem(y + r, NY) * span, span, 0) for r in (0, *ORDER)
    ]

    def to_owner(blocks, i):
        return shift(blocks[i + 1], "y", -ORDER[i], NY)

    def from_z(value, bit):
        return lax.ppermute(value, "dp", [(i, i ^ bit) for i in range(NZ)])

    spans_out, stats_c, out_got, query_mine = hold(spans_out, stats_c, out_got, query_mine)
    spans_in = [shift(v, "y", r, NY) for v, r in zip(spans_out[1:], ORDER)]
    out_back = swap(out_got, "x")
    grads_all = [grad_mine, grad_got, grad_mine_c, grad_got_c]
    rest = (grads_all, [stats, stats_c])
    got_grads = backward([query_mine, *queries_all[1:]], *rest, got_blocks, None)
    got_grads, spans_in, out_back = hold(got_grads, spans_in, out_back)

    z0, query_mine = hold(total_of(spans_out[0], spans_in), query_mine)
    z0_in = from_z(z0, 4)
    owned_got = [to_owner(got_grads, i) for i in range(3)]
    mine_grads = backward(
        [query_mine, *queries_all[1:]], *rest, mine_blocks, got_grads[RUN]
    )
    mine_grads, z0_in, out_mine = hold(mine_grads, z0_in, out_mine)
    dq_mine, dq_got, dq_other = mine_grads[RUN:]

    z1, out_mine, dq_other = hold(total_of(z0, [z0_in]), out_mine, dq_other)
    z1_in = from_z(z1, 1)
    dq_other = swap(dq_other, "c").astype(F32)
    attended = by_x(x, out_mine, out_back, 1)
    projected = dot(attended, out_weight, 1, 0)
    kept = lax.dynamic_slice_in_dim(projected, t * width, width, 1)
    leaving = lax.dynamic_slice_in_dim(projected, (1 - t) * width, width, 1).astype(BF)
    rows = dq_mine.shape[0]
    dq_got = (dq_got + dq_other[rows:]).astype(BF)
    z1_in, mine_leaving = hold(z1_in, mine_grads[1:3])

    z2 = total_of(z1, [z1_in])
    z2_in = from_z(z2, 2)
    arriving = swap(leaving, "tile")
    dq_back = swap(dq_got, "x")
    owned_mine = [shift(mine_leaving[i], "y", -ORDER[i], NY) for i in range(2)]
    z2_in, owned_got, arriving, dq_back = hold(z2_in, owned_got, arriving, dq_back)

    z4 = total_of(z2, [z2_in])
    spans_back = [shift(z4, "y", r, NY) for r in ORDER]
    z4_got = swap(z4, "x")
    back = swap(total_of(got_grads[0], owned_got), "x")
    spans_back, back, z4_got, leaving_far = hold(spans_back, back, z4_got, mine_grads[3])
    owned_mine.append(shift(leaving_far, "y", -ORDER[2], NY))
    spans_got, owned_mine = hold(swap(jnp.stack(spans_back), "x"), owned_mine)
    ours = jnp.stack([z4, *spans_back, z4_got, *[spans_got[i] for i in range(NY - 1)]])
    model = out_weight.shape[1]
    half = model // 2
    weight_gradient = jnp.zeros((width, model), F32)
    for cr, block in enumerate((ours, swap(ours, "c"))):
        column = (c + cr) % 2 * half
        for i, r in enumerate((0, *ORDER)):
            for xr in range(2):
                row = (x + xr) % 2 * group + lax.rem(y - r + NY, NY) * span
                weight_gradient = lax.dynamic_update_slice(
                    weight_gradient, block[xr * NY + i].astype(F32), (row, column)
                )

    layer_out = (residual[0].astype(F32) + kept + arriving.astype(F32)).astype(BF)
    total_mine = total_of(mine_grads[0], owned_mine)
    dq_mine = (dq_mine + dq_other[:rows]).astype(BF)
    grad_queries = by_x(x, dq_mine, dq_back, 1)
    grad_keys, grad_values = by_x(x, total_mine, back, 2)
    return (
        layer_out[None],
        grad_queries[None],
        grad_keys[None],
        grad_values[None],
        weight_gradient,
    )


def solution(mesh):
    fine = Mesh(mesh.devices.reshape(NZ, NY, 2, 2, 2), ("dp", "y", "x", "c", "tile"))
    rows = P("dp", ("y", "x", "c"), "tile")
    return jax.shard_map(
        body,
        mesh=fine,
        in_specs=(rows, rows, rows, rows, P("tile", None), rows),
        out_specs=(rows, rows, rows, rows, P("tile", None)),
        check_vma=False,
    )
```
